32 devices in a mesh: basin: 8 (over y, x, core), tm: 4 (over z).
Axes of the slice: x: 2, y: 2, z: 4, core: 2. Of those that a mesh axis runs over, the one named last changes fastest.
Arguments:
- inflow: float32 [128, 32768], P('tm', 'basin'), may hold values from 0.01 to 0.1
- cotangent: float32 [128, 16384], P('tm', 'basin'), may hold values from -6 to 6
- gauge_reach: int32 [16384], P('basin'), may hold values from 0 to 4095
- shape_param: float32 [32768], P('basin'), may hold values from 1.5 to 4
- scale_param: float32 [32768], P('basin'), may hold values from 1.5 to 10
- block_level: int32 [128], P('basin'), may hold values from 0 to 7, as said below
- down_local: int32 [32768], P('basin'), may hold values from -1 to 4095, as said below
- in_slot: int32 [32768], P('basin'), may hold values from -1 to 31, as said below
- send_reach: int32 [8, 7, 32], P('basin'), may hold values from -1 to 4095, as said below
Outputs:
- lateral_grad: float32 [128, 32768], P('tm', 'basin')
- param_grad: float32 [2, 32768], P(None, 'basin')
The draws below stay inside these ranges and needn't reach their ends.
Inputs may be any that keep to these rules, and one draw needn't show every extreme that they name: `block_level`: every partition holds between one and 4 blocks of each level, and exactly 4 blocks of some level. `down_local`: for a reach in a block of level h >= 1 whose in_slot is -1: a reach of the same partition in a block of level h - 1. -1 for reaches of level 0 and for reaches with in_slot >= 0. `in_slot`: A value s * 4 + c (s a partition other than the reach's own, c < 4) marks a reach of level h >= 1 fed by slot c that partition s fills for it at level h - 1; within one partition no value repeats among the reaches of one level. Exactly the slots that send_reach fills are received. send_reach[s, h, t * 4 + c] is a reach of partition s in a block of level h, or -1 for an empty slot; slots with t = s are empty. At some level some partition t receives all 4 slots from every other partition.
All inputs are finite; a program needn't handle non-finite values.
Results may differ from the reference program's by a relative error of at most 0.0003.
Values sent between devices are 32-bit elements; how exact they have to be, the bound alone decides.
No kernel may reach another device: no remote copies, remote signals or barrier semaphores. Data moves between devices by JAX's collectives and lax.ppermute only.
A program may use at most 128 MiB of HBM per device.

```python
import math
import jax
import jax.numpy as jnp

BLK = 256
BDEV = 16
LAGS = 30
LEVELS = 8
CAP = 4
MAXB = 4
REACHES = 32768
DAYS = 128
GAUGES = 16384
N_BASIN = 8


def topology(key):
    parts = N_BASIN
    per_device = BDEV * BLK
    keys = [jax.random.fold_in(key, 7000 + number) for number in range(12)]
    heavy = jax.random.randint(keys[0], (parts,), 0, LEVELS)
    offset = jax.random.randint(keys[1], (parts,), 0, LEVELS - 1)
    place = jnp.arange(BDEV, dtype=jnp.int32)[None, :]
    spread = jnp.where(place < MAXB + LEVELS - 1, place - MAXB, place - MAXB - LEVELS + 1 + offset[:, None]) % (LEVELS - 1)
    other = spread + (spread >= heavy[:, None]).astype(jnp.int32)
    base_level = jnp.where(place < MAXB, heavy[:, None], other)
    orders = jax.vmap(lambda sub: jax.random.permutation(sub, BDEV))(jax.random.split(keys[2], parts))
    levels = jnp.take_along_axis(base_level, orders, axis=1).astype(jnp.int32)
    level_ids = jnp.arange(LEVELS, dtype=jnp.int32)
    onehot = (levels[:, :, None] == level_ids[None, None, :]).astype(jnp.int32)
    counts = jnp.sum(onehot, axis=1)
    rank_own = jnp.sum((jnp.cumsum(onehot, axis=1) - 1) * onehot, axis=2)
    slot_ids = jnp.arange(MAXB, dtype=jnp.int32)
    block_ids = jnp.arange(BDEV, dtype=jnp.int32)
    matches = (levels[:, None, None, :] == level_ids[None, :, None, None]) & (rank_own[:, None, None, :] == slot_ids[None, None, :, None])
    table = jnp.sum(jnp.where(matches, block_ids[None, None, None, :], 0), axis=3)
    dev_grid = jnp.arange(parts, dtype=jnp.int32)[:, None, None]
    reach_level = jnp.broadcast_to(levels[:, :, None], (parts, BDEV, BLK))
    lower = jnp.maximum(reach_level - 1, 0)
    pick = jax.random.randint(keys[3], (parts, BDEV, BLK), 0, counts[dev_grid, lower])
    down_block = table[dev_grid, lower, pick]
    down_pos = jax.random.randint(keys[4], (parts, BDEV, BLK), 0, BLK)
    down = jnp.where(reach_level >= 1, down_block * BLK + down_pos, -1).reshape(parts * per_device)
    shape = (parts, LEVELS - 1, parts, CAP)
    src = jnp.arange(parts, dtype=jnp.int32)[:, None, None, None]
    lev = jnp.arange(LEVELS - 1, dtype=jnp.int32)[None, :, None, None]
    dst = jnp.arange(parts, dtype=jnp.int32)[None, None, :, None]
    cap_ids = jnp.arange(CAP, dtype=jnp.int32)[None, None, None, :]
    coin = jax.random.randint(keys[5], shape, 0, 2) == 1
    full_dst = jax.random.randint(keys[6], (), 0, parts)
    full_lev = jax.random.randint(keys[7], (), 0, LEVELS - 1)
    filled = (coin | (dst == full_dst) & (lev == full_lev)) & (src != dst)
    send_pick = jax.random.randint(keys[8], shape, 0, counts[src, lev])
    send_block = table[src, lev, send_pick]
    send_pos = jax.random.randint(keys[9], shape, 0, BLK)
    sends = jnp.where(filled, send_block * BLK + send_pos, -1).reshape(parts, LEVELS - 1, parts * CAP)
    recv_pick = jax.random.randint(keys[10], shape, 0, counts[dst, lev + 1])
    recv_block = table[dst, lev + 1, recv_pick]
    perm_keys = jax.random.split(keys[11], parts * (LEVELS - 1))
    perms = jax.vmap(lambda sub: jax.random.permutation(sub, BLK))(perm_keys).reshape(parts, LEVELS - 1, BLK).astype(jnp.int32)
    slot_value = src * CAP + cap_ids + 0 * lev + 0 * dst
    recv_pos = perms[dst, lev, slot_value]
    target = jnp.where(filled, dst * per_device + recv_block * BLK + recv_pos, parts * per_device)
    slots = jnp.full((parts * per_device,), -1, jnp.int32).at[target.reshape(-1)].set(slot_value.reshape(-1), mode='drop')
    down = jnp.where(slots >= 0, -1, down).astype(jnp.int32)
    return (levels.reshape(parts * BDEV), down, slots, sends.astype(jnp.int32))


def draw_block_level(key, part):
    return topology(key)[0]


def draw_down_local(key, part):
    return topology(key)[1]


def draw_in_slot(key, part):
    return topology(key)[2]


def draw_send_reach(key, part):
    return topology(key)[3]


def touch_ends(result, rng, least, largest):
    spot = [jax.random.randint(jax.random.fold_in(rng, axis), (), 0, length) for axis, length in enumerate(result.shape)]
    widest = result.shape.index(max(result.shape))
    neighbour = spot[:widest] + [(spot[widest] + 1) % result.shape[widest]] + spot[widest + 1:]
    return result.at[tuple(spot)].set(least).at[tuple(neighbour)].set(largest)


def shard_levels(own_key, extent, shards, smallest, largest):
    def one(dim, shards_of):
        draws = jax.random.uniform(jax.random.fold_in(jax.random.fold_in(own_key, 6), dim), (shards_of,), jnp.float32, smallest / len(shards), largest / len(shards))
        return jnp.repeat(jnp.exp(draws), extent[dim] // shards_of).reshape((-1,) + (1,) * (len(extent) - dim - 1))

    loudness = one(*shards[0])
    for cut in shards[1:]:
        loudness = loudness * one(*cut)
    return loudness


def centred(own_key, shape, width, reach, shards=(), held_as=jnp.bfloat16):
    drawn = width * jax.random.normal(own_key, shape, jnp.float32)
    if shards:
        drawn = drawn * shard_levels(own_key, shape, shards, -0.22, 0.18)
    return jnp.clip(drawn, -reach, reach).astype(held_as)


def setup_inputs(seed: int = 0) -> dict:
    splits = jax.random.split(jax.random.key(seed), 10)
    inflow = jnp.clip(jnp.exp(math.log(0.1) - 2.3025851 * jax.random.uniform(splits[0], (DAYS, REACHES), jnp.float32) ** shard_levels(splits[0], (DAYS, REACHES), ((0, 4), (1, 8)), -0.2, 0.2)), 0.01, 0.1)
    cotangent = centred(splits[1], (DAYS, GAUGES), 1.0, 6.0, ((0, 4), (1, 8)), jnp.float32)
    gauge_reach = touch_ends(jax.random.randint(splits[2], (GAUGES,), 0, BDEV * BLK), jax.random.fold_in(splits[2], 1), 0, (BDEV * BLK) - 1).astype(jnp.int32)
    shape_param = jnp.clip(1.5 + 2.5 * jax.random.uniform(splits[3], (REACHES,), jnp.float32) ** shard_levels(splits[3], (REACHES,), ((0, 8),), -0.2, 0.2), 1.5, 4.0)
    scale_param = jnp.clip(jnp.exp(math.log(10.0) - 1.89712 * jax.random.uniform(splits[4], (REACHES,), jnp.float32) ** shard_levels(splits[4], (REACHES,), ((0, 8),), -0.2, 0.2)), 1.5, 10.0)
    block_level = draw_block_level(jax.random.fold_in(splits[9], 71), 0)
    down_local = draw_down_local(jax.random.fold_in(splits[9], 71), 0)
    in_slot = draw_in_slot(jax.random.fold_in(splits[9], 71), 0)
    send_reach = draw_send_reach(jax.random.fold_in(splits[9], 71), 0)
    return {"inflow": inflow, "cotangent": cotangent, "gauge_reach": gauge_reach, "shape_param": shape_param, "scale_param": scale_param, "block_level": block_level, "down_local": down_local, "in_slot": in_slot, "send_reach": send_reach}


def kernel_of(shape_param, scale_param, lag_count):
    offsets = jnp.arange(lag_count, dtype=jnp.float32) + 0.5
    logits = (shape_param[None, :] - 1.0) * jnp.log(offsets)[:, None] - offsets[:, None] / scale_param[None, :]
    weights = jnp.exp(logits)
    return weights / jnp.sum(weights, axis=0, keepdims=True), offsets


def lag_adjoint(kernel, extended, day_count):
    summed = kernel[0][None, :] * extended[0:day_count]
    for lag_index in range(1, kernel.shape[0]):
        summed = summed + kernel[lag_index][None, :] * extended[lag_index:lag_index + day_count]
    return summed


def lag_gradient(adjoint_in, inflow_ext, lag_count, day_count):
    per_lag = []
    for lag_index in range(lag_count):
        first_day = lag_count - 1 - lag_index
        per_lag.append(jnp.sum(adjoint_in * inflow_ext[first_day:first_day + day_count], axis=0))
    return jnp.stack(per_lag)


def param_terms(kernel, offsets, scale_param, kernel_grad):
    weighted = jnp.sum(kernel * kernel_grad, axis=0, keepdims=True)
    logit_grad = kernel * (kernel_grad - weighted)
    shape_grad = jnp.sum(logit_grad * jnp.log(offsets)[:, None], axis=0)
    scale_grad = jnp.sum(logit_grad * offsets[:, None], axis=0) / (scale_param * scale_param)
    return jnp.stack([shape_grad, scale_grad])


def reference(inflow, cotangent, gauge_reach, shape_param, scale_param, block_level, down_local, in_slot, send_reach):
    day_count = inflow.shape[0]
    lag_count = LAGS
    per_device = BDEV * BLK
    kernel, offsets = kernel_of(shape_param, scale_param, lag_count)
    owners = (jnp.arange(GAUGES, dtype=jnp.int32) // (GAUGES // N_BASIN)) * per_device + gauge_reach
    gauge_seed = jnp.zeros((day_count, REACHES), jnp.float32).at[:, owners].add(cotangent)
    inflow_ext = jnp.concatenate([jnp.zeros((lag_count - 1, REACHES), jnp.float32), inflow], axis=0)
    device_base = jnp.arange(N_BASIN, dtype=jnp.int32) * per_device
    positions = jnp.arange(BLK, dtype=jnp.int32)
    slot_ids = jnp.arange(MAXB, dtype=jnp.int32)
    block_ids = jnp.arange(BDEV, dtype=jnp.int32)
    level_grid = block_level.reshape(N_BASIN, BDEV)
    owner_dev = jnp.repeat(jnp.arange(N_BASIN, dtype=jnp.int32), MAXB * BLK)
    adjoint_all = jnp.zeros((day_count, REACHES), jnp.float32)
    kernel_grad = jnp.zeros((lag_count, REACHES), jnp.float32)
    received = jnp.zeros((day_count, N_BASIN, N_BASIN * CAP), jnp.float32)
    for height in range(LEVELS):
        at_height = level_grid == height
        rank_of = jnp.cumsum(at_height.astype(jnp.int32), axis=1) - 1
        slot_hits = at_height[:, None, :] & (rank_of[:, None, :] == slot_ids[None, :, None])
        slot_valid = jnp.any(slot_hits, axis=2)
        chosen = jnp.sum(jnp.where(slot_hits, block_ids[None, None, :], 0), axis=2)
        local_cols = (chosen[:, :, None] * BLK + positions[None, None, :]).reshape(N_BASIN, MAXB * BLK)
        columns = (local_cols + device_base[:, None]).reshape(-1)
        below_reach = down_local[columns]
        local_part = jnp.where(below_reach[None, :] >= 0, adjoint_all[:, owner_dev * per_device + jnp.maximum(below_reach, 0)], 0.0)
        slot_of = in_slot[columns]
        remote_part = jnp.where(slot_of[None, :] >= 0, received[:, owner_dev, jnp.maximum(slot_of, 0)], 0.0)
        adjoint_in = gauge_seed[:, columns] + local_part + remote_part
        extended = jnp.concatenate([adjoint_in, jnp.zeros((lag_count - 1, adjoint_in.shape[1]), jnp.float32)], axis=0)
        outflow = lag_adjoint(kernel[:, columns], extended, day_count)
        lag_grads = lag_gradient(adjoint_in, inflow_ext[:, columns], lag_count, day_count)
        targets = jnp.where(jnp.repeat(slot_valid.reshape(-1), BLK), columns, REACHES)
        adjoint_all = adjoint_all.at[:, targets].set(outflow, mode="drop")
        kernel_grad = kernel_grad.at[:, targets].set(lag_grads, mode="drop")
        if height + 1 < LEVELS:
            wanted = send_reach[:, height, :]
            outgoing = jnp.where(wanted[None, :, :] >= 0, adjoint_all[:, device_base[:, None] + jnp.maximum(wanted, 0)], 0.0)
            received = outgoing.reshape(day_count, N_BASIN, N_BASIN, CAP).transpose(0, 2, 1, 3).reshape(day_count, N_BASIN, N_BASIN * CAP)
    param_grad = param_terms(kernel, offsets, scale_param, kernel_grad)
    return adjoint_all, param_grad
```

```python
import functools

import jax
import jax.numpy as jnp
from jax import lax
from jax.experimental import pallas as pl
from jax.experimental.pallas import tpu as pltpu
from jax.sharding import PartitionSpec as P

BLK = 256
LAGS = 30
LEVELS = 8
MAXB = 4
LANES = 128
KROWS = 32
SENDS = LEVELS - 1
F32 = jnp.float32
BF16 = jnp.bfloat16
VMEM_LIMIT = 56 * 1024 * 1024


def iota(shape, axis):
    return lax.broadcasted_iota(jnp.int32, shape, axis)


def split_terms(values):
    high = values.astype(BF16)
    return high, (values - high.astype(F32)).astype(BF16)


def one_hot(hits):
    return jnp.where(hits, 1.0, 0.0).astype(BF16)


def product(left, right):
    return jnp.dot(left, right, preferred_element_type=F32)


def list_blocks(level_ref, order_ref, count_ref):
    for height in range(LEVELS):
        count_ref[height] = 0

    @pl.loop(0, level_ref.shape[0])
    def _(block):
        height = level_ref[block]
        rank = count_ref[height]
        order_ref[height * MAXB + rank] = block
        count_ref[height] = rank + 1


def lag_weights(shape_row, scale_row):
    rows = iota((KROWS, shape_row.shape[1]), 0)
    offsets = rows.astype(F32) + 0.5
    logs = jnp.log(offsets)
    weights = jnp.exp((shape_row - 1.0) * logs - offsets / scale_row)
    weights = jnp.where(rows < LAGS, weights, 0.0)
    return weights / jnp.sum(weights, axis=0, keepdims=True), offsets, logs


def lag_sum(buf, chunk, weight_of, days, lags=LAGS):
    total = jnp.zeros((days, LANES), F32)
    for shift in range(8):
        steps = [k for k in range(shift, lags, 8)]
        shifted = buf[chunk, pl.ds(shift, days + 8 * (len(steps) - 1)), :]
        for step, lag in enumerate(steps):
            total = total + weight_of(lag) * shifted[8 * step : 8 * step + days]
    return total


def lag_sum_forward(buf, chunk, weights_of, days):
    totals = [jnp.zeros((days, LANES), F32) for _ in weights_of]
    for shift in range(8):
        shifted = buf[chunk, pl.ds(8 - shift, days + 24), :]
        for step in range(4):
            lag = 8 * step + shift
            if lag < LAGS:
                part = shifted[24 - 8 * step : 24 - 8 * step + days]
                totals = [t + w(lag) * part for t, w in zip(totals, weights_of)]
    return totals


def path_kernel(
    days, level_ref, part_ref, table_ref, want_ref, want_level_ref, node_ref, weight_ref, comp_ref,
    order_ref, count_ref, term_ref, buf_ref,
):
    list_blocks(level_ref, order_ref, count_ref)
    me = part_ref[0]
    width = want_ref.shape[1]
    want = want_ref[...]
    want_level = want_level_ref[...]
    below = jnp.full((1, width), -1, jnp.int32)
    parent = jnp.full((1, width), -1, jnp.int32)
    rows = iota((BLK, width), 0)
    krows = iota((KROWS, width), 0)
    node_ref[...] = jnp.full(node_ref.shape, -1, jnp.int32)
    for height in range(SENDS - 1, -1, -1):
        node = jnp.where((want_level == height) & (want >= 0), want, below)

        def gather(index, total, node=node, height=height):
            block = order_ref[height * MAXB + index]
            hits = jnp.where(rows == node - block * BLK, 1.0, 0.0)
            return total + jnp.dot(
                table_ref[block], hits, precision=lax.Precision.HIGHEST, preferred_element_type=F32
            )

        found = lax.fori_loop(0, count_ref[height], gather, jnp.zeros((8, width), F32))
        active = node >= 0
        down = jnp.round(found[0:1]).astype(jnp.int32)
        slot = jnp.round(found[1:2]).astype(jnp.int32)
        shape_row = jnp.where(active, found[2:3], 2.0)
        scale_row = jnp.where(active, found[3:4], 2.0)
        ends = active & (slot >= 0)
        below = jnp.where(active & (down >= 0), down, -1)
        sender = slot >> 2
        lane = (sender >> 2) * LANES + ((sender + (height - 1)) & 3) * KROWS + me * 4 + (slot & 3)
        parent = jnp.where(ends, (height - 1) * width + lane, parent)
        weights = lag_weights(shape_row, scale_row)[0]
        weights = jnp.where(active, weights, jnp.where(krows == 0, 1.0, 0.0))
        node_ref[height : height + 1, :] = node
        term_ref[height : height + 1, :] = jnp.where(ends, 1.0, 0.0)
        for chunk in range(width // LANES):
            weight_ref[height, chunk] = weights[:, chunk * LANES : (chunk + 1) * LANES]
    buf_ref[...] = jnp.zeros(buf_ref.shape, F32)
    first = iota((8, LANES), 0) == 0
    for height in range(1, SENDS):
        for chunk in range(width // LANES):
            ends = term_ref[height : height + 1, chunk * LANES : (chunk + 1) * LANES] > 0.5
            start = buf_ref[chunk, KROWS : KROWS + 8, :]
            buf_ref[chunk, KROWS : KROWS + 8, :] = jnp.where(first & ends, 1.0, start)

        @pl.loop(0, width // LANES)
        def _(chunk, height=height):
            row = lambda lag: weight_ref[height, chunk, pl.ds(lag, 1), :]
            (total,) = lag_sum_forward(buf_ref, chunk, [row], days)
            buf_ref[chunk, KROWS : KROWS + days, :] = total

    for chunk in range(width // LANES):
        lanes = slice(chunk * LANES, (chunk + 1) * LANES)
        comp_ref[0:days, lanes] = buf_ref[chunk, KROWS : KROWS + days, :]
    comp_ref[days : days + 8, :] = jnp.broadcast_to(parent.astype(F32), (8, width))


def weights_kernel(
    shape_ref, scale_ref, inflow_ref, earlier_ref, weight_ref, grad_ref, buf_ref, two_ref
):
    days = inflow_ref.shape[0]

    @pl.loop(0, shape_ref.shape[0])
    def _(block):
        scale_row = scale_ref[block]
        weights, offsets, logs = lag_weights(shape_ref[block], scale_row)
        by_shape = weights * (logs - jnp.sum(weights * logs, axis=0, keepdims=True))
        by_scale = weights * (offsets - jnp.sum(weights * offsets, axis=0, keepdims=True))
        by_scale = by_scale / (scale_row * scale_row)
        start = pl.multiple_of(block * BLK, BLK)
        for chunk in range(2):
            lanes = slice(chunk * LANES, (chunk + 1) * LANES)
            weight_ref[block, chunk] = weights[:, lanes]
            two_ref[chunk, 0] = by_shape[:, lanes]
            two_ref[chunk, 1] = by_scale[:, lanes]
            at = pl.ds(pl.multiple_of(start + chunk * LANES, LANES), LANES)
            buf_ref[chunk, 0:days, :] = earlier_ref[:, at]
            buf_ref[chunk, days : 2 * days, :] = inflow_ref[:, at]
        for chunk in range(2):
            rows = [
                lambda lag, chunk=chunk, which=which: two_ref[chunk, which, pl.ds(lag, 1), :]
                for which in range(2)
            ]
            first, second = lag_sum_forward(buf_ref, chunk, rows, days)
            lanes = slice(chunk * LANES, (chunk + 1) * LANES)
            grad_ref[block, 0, :, lanes] = first
            grad_ref[block, 1, :, lanes] = second


def gather_terms(pieces, terms_ref):
    shard_days = pieces[0].shape[0]
    days = shard_days * len(pieces)
    for number, piece in enumerate(pieces):
        high, low = split_terms(piece[...])
        terms_ref[number * shard_days : (number + 1) * shard_days, :] = high
        terms_ref[days + number * shard_days : days + (number + 1) * shard_days, :] = low


def gauge_product(terms_ref, gauge_ref, targets):
    gauges = gauge_ref.shape[0]
    total = jnp.zeros((terms_ref.shape[0], BLK), F32)
    for start in range(0, gauges, BLK):
        ids = gauge_ref[start : start + BLK, :]
        hits = jnp.concatenate(
            [one_hot(ids == targets[:, c * LANES : (c + 1) * LANES]) for c in range(2)], axis=1
        )
        total = total + product(terms_ref[:, start : start + BLK], hits)
    days = terms_ref.shape[0] // 2
    return total[:days] + total[days:]


def path_adjoint_kernel(shards, *refs):
    pieces = refs[:shards]
    gauge_ref, node_ref, weight_ref, out_ref, terms_ref, seed_ref, buf_ref = refs[shards:]
    days = out_ref.shape[0]
    gather_terms(pieces, terms_ref)

    @pl.loop(0, SENDS)
    def _(height):
        seeds = gauge_product(terms_ref, gauge_ref, node_ref[pl.ds(height, 1), :])
        for chunk in range(2):
            seed_ref[height, chunk] = seeds[:, chunk * LANES : (chunk + 1) * LANES]

    for chunk in range(2):
        buf_ref[chunk] = jnp.zeros(buf_ref.shape[1:], F32)

        @pl.loop(0, SENDS)
        def _(height, chunk=chunk):
            buf_ref[chunk, 0:days, :] = buf_ref[chunk, 0:days, :] + seed_ref[height, chunk]
            row = lambda lag: weight_ref[height, chunk, pl.ds(lag, 1), :]
            buf_ref[chunk, 0:days, :] = lag_sum(buf_ref, chunk, row, days)

        out_ref[:, chunk * LANES : (chunk + 1) * LANES] = buf_ref[chunk, 0:days, :]


def seed_kernel(shards, *refs):
    pieces = refs[:shards]
    gauge_ref, out_ref, terms_ref = refs[shards:]
    gather_terms(pieces, terms_ref)

    @pl.loop(0, out_ref.shape[0])
    def _(block):
        targets = iota((1, BLK), 1) + block * BLK
        out_ref[block] = gauge_product(terms_ref, gauge_ref, targets)


def full_kernel(
    own_days, level_ref, part_ref, a_own_ref, a_mate_ref, c_own_ref, c_mate_ref, seed_ref, weight_ref,
    grad_ref, down_ref, slot_ref, out_ref, param_ref,
    order_ref, count_ref, recv_ref, comp_ref, parent_buf, adj_ref, lat_ref,
):
    list_blocks(level_ref, order_ref, count_ref)
    me = part_ref[0]
    flip = (me >> 2) * LANES
    days = seed_ref.shape[1]
    width = 2 * LANES
    groups = iota((1, LANES), 1) >> 5
    rows = iota((BLK, width), 0)

    def merged(own_ref, mate_ref, height, half, at):
        lanes = slice((height // 4) * LANES, (height // 4 + 1) * LANES)
        total = None
        for ref, core in ((own_ref, 0), (mate_ref, 1)):
            for index in (2 * half, 2 * half + 1):
                sender = me ^ (core + 2 * index)
                part = ref[index, at, lanes]
                mine = groups == ((height + sender) & 3)
                total = part if total is None else jnp.where(mine, part, total)
        return total

    parent_buf[...] = jnp.zeros(parent_buf.shape, F32)
    for height in range(SENDS):
        if height:
            parents = jnp.concatenate(
                [
                    merged(c_own_ref, c_mate_ref, height, half, slice(days, days + 8))[0:1]
                    for half in range(2)
                ],
                axis=1,
            )
            parents = jnp.round(parents).astype(jnp.int32)
            parents = jnp.where(parents >= 0, parents ^ flip, -1)
            total = jnp.zeros((2 * days, width), F32)
            for lower in range(height):
                hits = one_hot(rows == parents - lower * width)
                total = total + product(recv_ref[lower], hits)
            total = total[:days] + total[days:]
            for half in range(2):
                parent_buf[half, 0:days, :] = total[:, half * LANES : (half + 1) * LANES]
                comp_ref[half] = merged(c_own_ref, c_mate_ref, height, half, slice(0, days))
        lags = min(days, (LAGS - 1) * height + 1)
        for half in range(2):
            result = merged(a_own_ref, a_mate_ref, height, half, slice(0, days))
            if height:
                tiles = [result[8 * i : 8 * i + 8] for i in range(days // 8)]
                for shift in range(8):
                    steps = [k for k in range(shift, lags, 8)]
                    for step, lag in enumerate(steps):
                        weight = comp_ref[half, lag : lag + 1, :]
                        for i in range(days // 8 - step):
                            at = 8 * (i + step) + shift
                            tiles[i] = tiles[i] + weight * parent_buf[half, at : at + 8, :]
                result = jnp.concatenate(tiles, axis=0)
            high, low = split_terms(result)
            lanes = slice(half * LANES, (half + 1) * LANES)
            recv_ref[height, 0:days, lanes] = high
            recv_ref[height, days : 2 * days, lanes] = low

    def days_of(height):
        return min(days, -(-(own_days + (LAGS - 1) * (LEVELS - 1 - height)) // 16) * 16)

    adj_ref[...] = jnp.zeros(adj_ref.shape, F32)
    for height in range(LEVELS):
        need = days_of(height)
        have = days_of(height - 1) if height else days

        @pl.loop(0, count_ref[height])
        def _(rank, height=height, need=need, have=have):
            block = order_ref[height * MAXB + rank]
            adjoint = seed_ref[block, 0:have, :]
            if height:
                slot = slot_ref[block]
                sender = slot >> 2
                lane = ((sender >> 2) * LANES ^ flip) + ((sender + (height - 1)) & 3) * KROWS
                lane = jnp.where(slot >= 0, lane + me * 4 + (slot & 3), -1)
                hits = one_hot(rows == lane)
                if have == days:
                    total = product(recv_ref[height - 1], hits)
                else:
                    total = jnp.concatenate(
                        [
                            product(recv_ref[height - 1, 0:have, :], hits),
                            product(recv_ref[height - 1, days : days + have, :], hits),
                        ],
                        axis=0,
                    )
                down = down_ref[block]

                def gather(index, total):
                    source = order_ref[(height - 1) * MAXB + index]
                    hits = one_hot(rows == down - source * BLK)
                    return total + product(lat_ref[source, 0 : 2 * have, :], hits)

                total = lax.fori_loop(0, count_ref[height - 1], gather, total)
                adjoint = adjoint + total[:have] + total[have:]
            at = pl.ds(pl.multiple_of(block * BLK, BLK), BLK)
            param_ref[0:1, at] = jnp.sum(adjoint[:own_days] * grad_ref[block, 0], axis=0, keepdims=True)
            param_ref[1:2, at] = jnp.sum(adjoint[:own_days] * grad_ref[block, 1], axis=0, keepdims=True)
            for chunk in range(2):
                adj_ref[chunk, 0:have, :] = adjoint[:, chunk * LANES : (chunk + 1) * LANES]

            for chunk in range(2):
                row = lambda lag, chunk=chunk: weight_ref[block, chunk, pl.ds(lag, 1), :]
                result = lag_sum(adj_ref, chunk, row, need)
                at = pl.ds(pl.multiple_of(block * BLK + chunk * LANES, LANES), LANES)
                out_ref[:, at] = result[:own_days]
                if height + 1 < LEVELS:
                    high, low = split_terms(result)
                    lanes = slice(chunk * LANES, (chunk + 1) * LANES)
                    lat_ref[block, 0:need, lanes] = high
                    lat_ref[block, need : 2 * need, lanes] = low


def call(kernel, out_shape, in_smem, in_vmem, scratch, flops):
    vmem = pl.BlockSpec(memory_space=pltpu.VMEM)
    smem = pl.BlockSpec(memory_space=pltpu.SMEM)
    size = lambda leaves: sum(leaf.size * leaf.dtype.itemsize for leaf in leaves)
    return pl.pallas_call(
        kernel,
        out_shape=out_shape,
        in_specs=[smem] * len(in_smem) + [vmem] * len(in_vmem),
        out_specs=jax.tree.map(lambda _: vmem, out_shape),
        scratch_shapes=scratch,
        compiler_params=pltpu.CompilerParams(vmem_limit_bytes=VMEM_LIMIT),
        cost_estimate=pl.CostEstimate(
            flops=flops,
            bytes_accessed=size(in_vmem) + size(jax.tree.leaves(out_shape)),
            transcendentals=0,
        ),
    )(*in_smem, *in_vmem)


def exchange(values, axis, by):
    return lax.ppermute(values, axis, [(i, i ^ by) for i in range(lax.axis_size(axis))])


def over_basin(values):
    others = [exchange(values, "basin", by) for by in (2, 4, 6)]
    own = jnp.stack([values] + others)
    return own, exchange(own, "basin", 1)


def fast_shards(
    inflow, cotangent, gauge_reach, shape_param, scale_param, block_level, down_local, in_slot, send_reach,
):
    own_days, reaches = inflow.shape
    gauges = cotangent.shape[1]
    blocks = block_level.shape[0]
    shards = lax.axis_size("tm")
    days = shards * own_days
    width = 2 * LANES
    me = lax.axis_index("basin")
    part = me.astype(jnp.int32).reshape(1)
    earlier = lax.ppermute(inflow, "tm", [(i, i + 1) for i in range(shards - 1)])
    pieces = [cotangent] + [
        lax.ppermute(cotangent, "tm", [(i + by, i) for i in range(shards - by)]) for by in range(1, shards)
    ]
    turn = (4 - me % 4) % 4
    padded = jnp.concatenate([send_reach[0], jnp.full((1, send_reach.shape[2]), -1, jnp.int32)], axis=0)
    padded = padded.reshape(2, 4, KROWS)
    padded = jnp.concatenate([padded, padded], axis=1)
    want = lax.dynamic_slice(padded, (0, turn, 0), (2, 4, KROWS)).reshape(1, width)
    lane = jnp.arange(width, dtype=jnp.int32)
    want_level = ((lane // LANES) * 4 + ((lane % LANES) // KROWS + turn) % 4).reshape(1, width)
    zero = jnp.zeros_like(shape_param)
    table = jnp.stack(
        [down_local.astype(F32), in_slot.astype(F32), shape_param, scale_param, zero, zero, zero, zero]
    )
    table = table.reshape(8, blocks, BLK).transpose(1, 0, 2)
    gauge_ids = jnp.broadcast_to(gauge_reach[:, None], (gauges, LANES))
    by_block = lambda values: values.reshape(blocks, 1, BLK)
    shape_of = jax.ShapeDtypeStruct
    tables = [pltpu.SMEM((LEVELS * MAXB,), jnp.int32), pltpu.SMEM((LEVELS,), jnp.int32)]

    nodes, path_weights, composed = call(
        functools.partial(path_kernel, days),
        (
            shape_of((8, width), jnp.int32),
            shape_of((SENDS, 2, KROWS, LANES), F32),
            shape_of((days + 8, width), F32),
        ),
        [block_level, part],
        [table, want, want_level],
        tables + [pltpu.VMEM((8, width), F32), pltpu.VMEM((2, KROWS + days, LANES), F32)],
        8_000_000_000,
    )
    c_own, c_mate = over_basin(composed)
    weights, grads = call(
        weights_kernel,
        (shape_of((blocks, 2, KROWS, LANES), F32), shape_of((blocks, 2, own_days, BLK), F32)),
        [],
        [by_block(shape_param), by_block(scale_param), inflow, earlier],
        [pltpu.VMEM((2, 2 * own_days, LANES), F32), pltpu.VMEM((2, 2, KROWS, LANES), F32)],
        4_000_000_000,
    )
    terms = pltpu.VMEM((2 * days, gauges), BF16)
    path_adjoint = call(
        functools.partial(path_adjoint_kernel, shards),
        shape_of((days, width), F32),
        [],
        pieces + [gauge_ids, nodes, path_weights],
        [terms, pltpu.VMEM((SENDS, 2, days, LANES), F32), pltpu.VMEM((2, days + KROWS, LANES), F32)],
        4_000_000_000,
    )
    a_own, a_mate = over_basin(path_adjoint)
    seeds = call(
        functools.partial(seed_kernel, shards),
        shape_of((blocks, days, BLK), F32),
        [],
        pieces + [gauge_ids],
        [terms],
        6_000_000_000,
    )
    lateral, params = call(
        functools.partial(full_kernel, own_days),
        (shape_of((own_days, reaches), F32), shape_of((2, reaches), F32)),
        [block_level, part],
        [a_own, a_mate, c_own, c_mate, seeds, weights, grads, by_block(down_local), by_block(in_slot)],
        tables
        + [
            pltpu.VMEM((SENDS, 2 * days, width), BF16),
            pltpu.VMEM((2, days, LANES), F32),
            pltpu.VMEM((2, 2 * days, LANES), F32),
            pltpu.VMEM((2, days + KROWS, LANES), F32),
            pltpu.VMEM((blocks, 2 * days, BLK), BF16),
        ],
        10_000_000_000,
    )
    first, second, third = (exchange(params, "tm", by) for by in (1, 2, 3))
    return lateral, (params + first) + (second + third)


def passed_along(shard, axis, by):
    peers = lax.axis_size(axis)
    pairs = [(i, i + by) for i in range(peers) if 0 <= i + by < peers]
    return lax.ppermute(shard, axis, pairs)


def kernel_of(shape_param, scale_param, lag_count):
    offsets = jnp.arange(lag_count, dtype=jnp.float32) + 0.5
    logits = (shape_param[None, :] - 1.0) * jnp.log(offsets)[:, None] - offsets[
        :, None
    ] / scale_param[None, :]
    weights = jnp.exp(logits)
    return (weights / jnp.sum(weights, axis=0, keepdims=True), offsets)


def lag_adjoint(kernel, extended, day_count):
    summed = kernel[0][None, :] * extended[0:day_count]
    for lag_index in range(1, kernel.shape[0]):
        summed = summed + kernel[lag_index][None, :] * extended[lag_index : lag_index + day_count]
    return summed


def lag_gradient(adjoint_in, inflow_ext, lag_count, day_count):
    per_lag = []
    for lag_index in range(lag_count):
        first_day = lag_count - 1 - lag_index
        per_lag.append(jnp.sum(adjoint_in * inflow_ext[first_day : first_day + day_count], axis=0))
    return jnp.stack(per_lag)


def param_terms(kernel, offsets, scale_param, kernel_grad):
    weighted = jnp.sum(kernel * kernel_grad, axis=0, keepdims=True)
    logit_grad = kernel * (kernel_grad - weighted)
    shape_grad = jnp.sum(logit_grad * jnp.log(offsets)[:, None], axis=0)
    scale_grad = jnp.sum(logit_grad * offsets[:, None], axis=0) / (scale_param * scale_param)
    return jnp.stack([shape_grad, scale_grad])


def take_blocks(values, chosen, block_count):
    rows = values.shape[0]
    picked = jnp.take(values.reshape(rows, block_count, BLK), chosen, axis=1)
    return picked.reshape(rows, chosen.shape[0] * BLK)


def inbound(seed_part, adjoint_all, received, below_reach, slot_of):
    local_part = jnp.where(
        below_reach[None, :] >= 0, adjoint_all[:, jnp.maximum(below_reach, 0)], 0.0
    )
    remote_part = jnp.where(slot_of[None, :] >= 0, received[:, jnp.maximum(slot_of, 0)], 0.0)
    return seed_part + local_part + remote_part


def shards(
    inflow,
    cotangent,
    gauge_reach,
    shape_param,
    scale_param,
    block_level,
    down_local,
    in_slot,
    send_reach,
):
    day_count, reach_count = inflow.shape
    lag_count = LAGS
    block_count = block_level.shape[0]
    kernel, offsets = kernel_of(shape_param, scale_param, lag_count)
    gauge_seed = jnp.zeros((day_count, reach_count), jnp.float32).at[:, gauge_reach].add(cotangent)
    earlier = passed_along(inflow[day_count - (lag_count - 1) :], "tm", 1)
    inflow_ext = jnp.concatenate([earlier, inflow], axis=0)
    adjoint_all = jnp.zeros((day_count, reach_count), jnp.float32)
    kernel_grad = jnp.zeros((lag_count, reach_count), jnp.float32)
    received = jnp.zeros((day_count, send_reach.shape[2]), jnp.float32)
    slot_ids = jnp.arange(MAXB, dtype=jnp.int32)
    block_ids = jnp.arange(block_count, dtype=jnp.int32)
    down_rows = down_local.reshape(1, reach_count)
    slot_rows = in_slot.reshape(1, reach_count)
    for height in range(LEVELS):
        at_height = block_level == height
        rank_of = jnp.cumsum(at_height.astype(jnp.int32)) - 1
        slot_hits = at_height[None, :] & (rank_of[None, :] == slot_ids[:, None])
        slot_valid = jnp.any(slot_hits, axis=1)
        chosen = jnp.sum(jnp.where(slot_hits, block_ids[None, :], 0), axis=1)
        below_reach = take_blocks(down_rows, chosen, block_count)[0]
        slot_of = take_blocks(slot_rows, chosen, block_count)[0]
        seed_part = take_blocks(gauge_seed, chosen, block_count)
        adjoint_in = inbound(seed_part, adjoint_all, received, below_reach, slot_of)
        later_head = passed_along(adjoint_in[: lag_count - 1], "tm", -1)
        extended = jnp.concatenate([adjoint_in, later_head], axis=0)
        outflow = lag_adjoint(take_blocks(kernel, chosen, block_count), extended, day_count)
        lag_grads = lag_gradient(
            adjoint_in, take_blocks(inflow_ext, chosen, block_count), lag_count, day_count
        )
        target_blocks = jnp.where(slot_valid, chosen, block_count)
        adjoint_all = (
            adjoint_all.reshape(day_count, block_count, BLK)
            .at[:, target_blocks]
            .set(outflow.reshape(day_count, MAXB, BLK), mode="drop")
            .reshape(day_count, reach_count)
        )
        kernel_grad = (
            kernel_grad.reshape(lag_count, block_count, BLK)
            .at[:, target_blocks]
            .set(lag_grads.reshape(lag_count, MAXB, BLK), mode="drop")
            .reshape(lag_count, reach_count)
        )
        if height + 1 < LEVELS:
            wanted = send_reach[0, height]
            outgoing = jnp.where(wanted[None, :] >= 0, adjoint_all[:, jnp.maximum(wanted, 0)], 0.0)
            received = lax.all_to_all(outgoing, "basin", split_axis=1, concat_axis=1, tiled=True)
    kernel_total = lax.psum(kernel_grad, "tm")
    param_grad = param_terms(kernel, offsets, scale_param, kernel_total)
    return (adjoint_all, param_grad)


def solution(mesh):
    in_specs = (
        P("tm", "basin"),
        P("tm", "basin"),
        P("basin"),
        P("basin"),
        P("basin"),
        P("basin"),
        P("basin"),
        P("basin"),
        P("basin", None, None),
    )
    out_specs = (P("tm", "basin"), P(None, "basin"))
    small = mesh.shape["basin"] == 8 and mesh.shape["tm"] == 4
    body = fast_shards if small else shards
    return jax.shard_map(body, mesh=mesh, in_specs=in_specs, out_specs=out_specs, check_vma=False)
```

```python
import functools

import jax
import jax.numpy as jnp
from jax import lax
from jax.experimental import pallas as pl
from jax.experimental.pallas import tpu as pltpu
from jax.sharding import PartitionSpec as P

BLK = 256
LAGS = 30
LEVELS = 8
MAXB = 4
LANES = 128
KROWS = 32
SENDS = LEVELS - 1
WIDTH = 2 * LANES
F32 = jnp.float32
BF16 = jnp.bfloat16
VMEM_LIMIT = 20 * 1024 * 1024


def iota(shape, axis):
    return lax.broadcasted_iota(jnp.int32, shape, axis)


def split_terms(values):
    high = values.astype(BF16)
    return high, (values - high.astype(F32)).astype(BF16)


def one_hot(hits):
    return jnp.where(hits, 1.0, 0.0).astype(BF16)


def product(left, right):
    return jnp.dot(left, right, preferred_element_type=F32)


def list_blocks(level_ref, order_ref, count_ref):
    for height in range(LEVELS):
        count_ref[height] = 0

    @pl.loop(0, level_ref.shape[0])
    def _(block):
        height = level_ref[block]
        rank = count_ref[height]
        order_ref[height * MAXB + rank] = block
        count_ref[height] = rank + 1


def lag_weights(shape_row, scale_row):
    rows = iota((KROWS, shape_row.shape[1]), 0)
    offsets = rows.astype(F32) + 0.5
    logs = jnp.log(offsets)
    weights = jnp.exp((shape_row - 1.0) * logs - offsets / scale_row)
    weights = jnp.where(rows < LAGS, weights, 0.0)
    return weights / jnp.sum(weights, axis=0, keepdims=True), offsets, logs


def lag_sum(buf, chunk, weight_of, days, lags=LAGS):
    total = jnp.zeros((days, LANES), F32)
    for shift in range(8):
        steps = [k for k in range(shift, lags, 8)]
        shifted = buf[chunk, pl.ds(shift, days + 8 * (len(steps) - 1)), :]
        for step, lag in enumerate(steps):
            total = total + weight_of(lag) * shifted[8 * step : 8 * step + days]
    return total


def lag_sums(buf, chunk, weight_ref, inflow, days):
    own_days = inflow.shape[0]
    total = jnp.zeros((days, LANES), F32)
    parts = [jnp.zeros((8, LANES), F32) for _ in range(2)]
    for shift in range(8):
        steps = [k for k in range(shift, LAGS, 8)]
        shifted = buf[chunk, pl.ds(shift, days + 8 * (len(steps) - 1)), :]
        for step, lag in enumerate(steps):
            total = total + weight_ref[0, lag : lag + 1, :] * shifted[8 * step : 8 * step + days]
            grad = inflow * shifted[8 * step : 8 * step + own_days]
            grad = sum(grad[i : i + 8] for i in range(0, own_days, 8))
            parts = [p + weight_ref[1 + w, lag : lag + 1, :] * grad for w, p in enumerate(parts)]
    return total, jnp.concatenate([jnp.sum(p, axis=0, keepdims=True) for p in parts], axis=0)


def lag_sum_forward(buf, chunk, weights_of, days):
    totals = [jnp.zeros((days, LANES), F32) for _ in weights_of]
    for shift in range(8):
        shifted = buf[chunk, pl.ds(8 - shift, days + 24), :]
        for step in range(4):
            lag = 8 * step + shift
            if lag < LAGS:
                part = shifted[24 - 8 * step : 24 - 8 * step + days]
                totals = [t + w(lag) * part for t, w in zip(totals, weights_of)]
    return totals


def fill_weights(shape_ref, scale_ref, weight_ref):
    @pl.loop(0, shape_ref.shape[0])
    def _(block):
        scale_row = scale_ref[block]
        weights, offsets, logs = lag_weights(shape_ref[block], scale_row)
        by_shape = weights * (logs - jnp.sum(weights * logs, axis=0, keepdims=True))
        by_scale = weights * (offsets - jnp.sum(weights * offsets, axis=0, keepdims=True))
        by_scale = by_scale / (scale_row * scale_row)
        for chunk in range(2):
            lanes = slice(chunk * LANES, (chunk + 1) * LANES)
            for which, rows in enumerate((weights, by_shape, by_scale)):
                weight_ref[block, chunk, which] = rows[:, lanes]


def path_kernel(
    days, level_ref, part_ref, down_ref, slot_ref, shape_ref, scale_ref, send_ref, node_ref, weight_ref,
    comp_ref, reach_weight_ref, order_ref, count_ref, term_ref, buf_ref,
):
    fill_weights(shape_ref, scale_ref, reach_weight_ref)
    list_blocks(level_ref, order_ref, count_ref)
    me = part_ref[0]
    width = WIDTH
    turn = me & 3
    halves = []
    for half in range(2):
        listed = [
            send_ref[h] if h < SENDS else jnp.full((1, KROWS), -1, jnp.int32)
            for h in range(4 * half, 4 * half + 4)
        ]
        listed = jnp.broadcast_to(jnp.concatenate(listed, axis=1), (8, LANES))
        halves.append(pltpu.roll(listed, turn * KROWS, 1)[0:1])
    want = jnp.concatenate(halves, axis=1)
    lane_id = iota((1, width), 1)
    want_level = (lane_id >> 7) * 4 + ((((lane_id & (LANES - 1)) >> 5) - turn) & 3)
    blank = jnp.zeros((4, BLK), F32)
    below = jnp.full((1, width), -1, jnp.int32)
    parent = jnp.full((1, width), -1, jnp.int32)
    rows = iota((BLK, width), 0)
    krows = iota((KROWS, width), 0)
    node_ref[...] = jnp.full(node_ref.shape, -1, jnp.int32)
    for height in range(SENDS - 1, -1, -1):
        node = jnp.where((want_level == height) & (want >= 0), want, below)

        def gather(index, total, node=node, height=height):
            block = order_ref[height * MAXB + index]
            hits = one_hot(rows == node - block * BLK)
            table = jnp.concatenate(
                [
                    down_ref[block].astype(F32),
                    slot_ref[block].astype(F32),
                    shape_ref[block],
                    scale_ref[block],
                    blank,
                ],
                axis=0,
            )
            high = table.astype(BF16)
            rest = table - high.astype(F32)
            middle = rest.astype(BF16)
            low = (rest - middle.astype(F32)).astype(BF16)
            return total + product(jnp.concatenate([high, middle, low, high * 0], axis=0), hits)

        found = lax.fori_loop(0, count_ref[height], gather, jnp.zeros((32, width), F32))
        found = (found[0:8] + found[8:16]) + found[16:24]
        active = node >= 0
        down = jnp.round(found[0:1]).astype(jnp.int32)
        slot = jnp.round(found[1:2]).astype(jnp.int32)
        shape_row = jnp.where(active, found[2:3], 2.0)
        scale_row = jnp.where(active, found[3:4], 2.0)
        ends = active & (slot >= 0)
        below = jnp.where(active & (down >= 0), down, -1)
        sender = slot >> 2
        lane = (sender >> 2) * LANES + ((sender + (height - 1)) & 3) * KROWS + me * 4 + (slot & 3)
        parent = jnp.where(ends, (height - 1) * width + lane, parent)
        weights = lag_weights(shape_row, scale_row)[0]
        weights = jnp.where(active, weights, jnp.where(krows == 0, 1.0, 0.0))
        node_ref[height : height + 1, :] = node
        term_ref[height : height + 1, :] = jnp.where(ends, 1.0, 0.0)
        for chunk in range(width // LANES):
            weight_ref[height, chunk] = weights[:, chunk * LANES : (chunk + 1) * LANES]
    buf_ref[...] = jnp.zeros(buf_ref.shape, F32)
    first = iota((8, LANES), 0) == 0
    for height in range(1, SENDS):
        for chunk in range(height // 4, width // LANES):
            ends = term_ref[height : height + 1, chunk * LANES : (chunk + 1) * LANES] > 0.5
            start = buf_ref[chunk, KROWS : KROWS + 8, :]
            buf_ref[chunk, KROWS : KROWS + 8, :] = jnp.where(first & ends, 1.0, start)

        @pl.loop(height // 4, width // LANES)
        def _(chunk, height=height):
            row = lambda lag: weight_ref[height, chunk, pl.ds(lag, 1), :]
            (total,) = lag_sum_forward(buf_ref, chunk, [row], days)
            buf_ref[chunk, KROWS : KROWS + days, :] = total

    for chunk in range(width // LANES):
        lanes = slice(chunk * LANES, (chunk + 1) * LANES)
        comp_ref[0:days, lanes] = buf_ref[chunk, KROWS : KROWS + days, :]
    comp_ref[days : days + 8, :] = jnp.broadcast_to(parent.astype(F32), (8, width))


def gather_terms(pieces, terms_ref):
    shard_days = pieces[0].shape[0]
    days = shard_days * len(pieces)
    for number, piece in enumerate(pieces):
        high, low = split_terms(piece[...])
        terms_ref[number * shard_days : (number + 1) * shard_days, :] = high
        terms_ref[days + number * shard_days : days + (number + 1) * shard_days, :] = low


def gauge_product(terms_ref, gauge_ref, targets):
    gauges = gauge_ref.shape[0]
    total = jnp.zeros((terms_ref.shape[0], BLK), F32)
    for start in range(0, gauges, BLK):
        ids = gauge_ref[start : start + BLK, :]
        hits = jnp.concatenate(
            [one_hot(ids == targets[:, c * LANES : (c + 1) * LANES]) for c in range(2)], axis=1
        )
        total = total + product(terms_ref[:, start : start + BLK], hits)
    days = terms_ref.shape[0] // 2
    return total[:days] + total[days:]


def path_adjoint_kernel(shards, *refs):
    pieces = refs[:shards]
    gauge_ref, node_ref, weight_ref, out_ref, terms_ref, seed_ref, buf_ref = refs[shards:]
    days = out_ref.shape[0]
    gather_terms(pieces, terms_ref)

    @pl.loop(0, SENDS)
    def _(height):
        seeds = gauge_product(terms_ref, gauge_ref, node_ref[pl.ds(height, 1), :])
        for chunk in range(2):
            seed_ref[height, chunk] = seeds[:, chunk * LANES : (chunk + 1) * LANES]

    for chunk in range(2):
        buf_ref[chunk] = jnp.zeros(buf_ref.shape[1:], F32)

        @pl.loop(0, min(SENDS, 4 * chunk + 4))
        def _(height, chunk=chunk):
            buf_ref[chunk, 0:days, :] = buf_ref[chunk, 0:days, :] + seed_ref[height, chunk]
            row = lambda lag: weight_ref[height, chunk, pl.ds(lag, 1), :]
            buf_ref[chunk, 0:days, :] = lag_sum(buf_ref, chunk, row, days)

        out_ref[:, chunk * LANES : (chunk + 1) * LANES] = buf_ref[chunk, 0:days, :]


def seed_kernel(shards, first, *refs):
    pieces = refs[:shards]
    gauge_ref, out_ref, terms_ref = refs[shards:]
    gather_terms(pieces, terms_ref)

    @pl.loop(0, out_ref.shape[0])
    def _(block):
        targets = iota((1, BLK), 1) + (first + block) * BLK
        out_ref[block] = gauge_product(terms_ref, gauge_ref, targets)


def full_kernel(
    own_days, level_ref, part_ref, a_own_ref, a_mate_ref, c_own_ref, c_mate_ref, first_seed_ref, last_seed_ref,
    weight_ref, inflow_ref, down_ref, slot_ref, out_ref, param_ref,
    order_ref, count_ref, recv_ref, comp_ref, parent_buf, adj_ref, lat_ref,
):
    list_blocks(level_ref, order_ref, count_ref)
    me = part_ref[0]
    flip = (me >> 2) * LANES
    first_blocks, days = first_seed_ref.shape[:2]
    width = 2 * LANES
    groups = iota((1, LANES), 1) >> 5
    rows = iota((BLK, width), 0)

    def merged(own_ref, mate_ref, height, half, at):
        lanes = slice((height // 4) * LANES, (height // 4 + 1) * LANES)
        total = None
        for ref, core in ((own_ref, 0), (mate_ref, 1)):
            for index in (2 * half, 2 * half + 1):
                sender = me ^ (core + 2 * index)
                part = ref[index, at, lanes]
                mine = groups == ((height + sender) & 3)
                total = part if total is None else jnp.where(mine, part, total)
        return total

    def days_of(height):
        return min(days, -(-(own_days + (LAGS - 1) * (LEVELS - 1 - height)) // 16) * 16)

    parent_buf[...] = jnp.zeros(parent_buf.shape, F32)
    for height in range(SENDS):
        if height:
            parents = jnp.concatenate(
                [
                    merged(c_own_ref, c_mate_ref, height, half, slice(days, days + 8))[0:1]
                    for half in range(2)
                ],
                axis=1,
            )
            parents = jnp.round(parents).astype(jnp.int32)
            parents = jnp.where(parents >= 0, parents ^ flip, -1)
            hits = jnp.concatenate(
                [one_hot(rows == parents - lower * width) for lower in range(height)], axis=0
            )
            total = product(recv_ref[:, 0 : height * width], hits)
            total = total[:days] + total[days:]
            for half in range(2):
                parent_buf[half, 0:days, :] = total[:, half * LANES : (half + 1) * LANES]
                comp_ref[half] = merged(c_own_ref, c_mate_ref, height, half, slice(0, days))
        lags = min(days, (LAGS - 1) * height + 1)
        for half in range(2):
            result = merged(a_own_ref, a_mate_ref, height, half, slice(0, days))
            if height:
                count = days_of(height) // 8
                tiles = [result[8 * i : 8 * i + 8] for i in range(days // 8)]
                for shift in range(8):
                    steps = [k for k in range(shift, lags, 8)]
                    for step, lag in enumerate(steps):
                        weight = comp_ref[half, lag : lag + 1, :]
                        for i in range(min(count, days // 8 - step)):
                            at = 8 * (i + step) + shift
                            tiles[i] = tiles[i] + weight * parent_buf[half, at : at + 8, :]
                result = jnp.concatenate(tiles, axis=0)
            high, low = split_terms(result)
            lanes = slice(height * width + half * LANES, height * width + (half + 1) * LANES)
            recv_ref[0:days, lanes] = high
            recv_ref[days : 2 * days, lanes] = low

    adj_ref[...] = jnp.zeros(adj_ref.shape, F32)
    for height in range(LEVELS):
        need = days_of(height)
        have = days_of(height - 1) if height else days

        @pl.loop(0, count_ref[height])
        def _(rank, height=height, need=need, have=have):
            block = order_ref[height * MAXB + rank]

            def keep(adjoint):
                for chunk in range(2):
                    adj_ref[chunk, 0:have, :] = adjoint[:, chunk * LANES : (chunk + 1) * LANES]

            @pl.when(block < first_blocks)
            def _():
                keep(first_seed_ref[block, 0:have, :])

            @pl.when(block >= first_blocks)
            def _():
                keep(last_seed_ref[block - first_blocks, 0:have, :])

            if height:
                slot = slot_ref[block]
                sender = slot >> 2
                lane = ((sender >> 2) * LANES ^ flip) + ((sender + (height - 1)) & 3) * KROWS
                lane = jnp.where(slot >= 0, lane + me * 4 + (slot & 3), -1)
                down = down_ref[block]
                at = slice((height - 1) * width, height * width)

                def gather(sources):
                    hits = [one_hot(rows == lane)]
                    for index in range(sources):
                        source = order_ref[(height - 1) * MAXB + index]
                        hits.append(one_hot(rows == down - source * BLK))
                    terms = []
                    for start, first in ((0, 0), (have, days)):
                        local = lat_ref[(height - 1) % 2, start : start + have, 0 : sources * BLK]
                        received = recv_ref[first : first + have, at]
                        terms.append(jnp.concatenate([received, local], axis=1))
                    total = product(jnp.concatenate(terms, axis=0), jnp.concatenate(hits, axis=0))
                    seeds = jnp.concatenate([adj_ref[chunk, 0:have, :] for chunk in range(2)], axis=1)
                    keep(seeds + total[:have] + total[have:])

                for sources in range(1, MAXB + 1):
                    pl.when(count_ref[height - 1] == sources)(functools.partial(gather, sources))
            for chunk in range(2):
                at = pl.ds(pl.multiple_of(block * BLK + chunk * LANES, LANES), LANES)
                result, params = lag_sums(adj_ref, chunk, weight_ref.at[block, chunk], inflow_ref[:, at], need)
                out_ref[:, at] = result[:own_days]
                param_ref[:, at] = params
                if height + 1 < LEVELS:
                    high, low = split_terms(result)
                    lanes = pl.ds(pl.multiple_of(rank * BLK + chunk * LANES, LANES), LANES)
                    lat_ref[height % 2, 0:need, lanes] = high
                    lat_ref[height % 2, need : 2 * need, lanes] = low


def call(kernel, out_shape, in_smem, in_vmem, scratch, flops, limit=VMEM_LIMIT):
    vmem = pl.BlockSpec(memory_space=pltpu.VMEM)
    smem = pl.BlockSpec(memory_space=pltpu.SMEM)
    return pl.pallas_call(
        kernel,
        out_shape=out_shape,
        in_specs=[smem] * len(in_smem) + [vmem] * len(in_vmem),
        out_specs=jax.tree.map(lambda _: vmem, out_shape),
        scratch_shapes=scratch,
        compiler_params=pltpu.CompilerParams(vmem_limit_bytes=limit),
        cost_estimate=pl.CostEstimate(
            flops=flops,
            bytes_accessed=flops // 1000,
            transcendentals=0,
        ),
    )(*in_smem, *in_vmem)


def exchange(values, axis, by):
    return lax.ppermute(values, axis, [(i, i ^ by) for i in range(lax.axis_size(axis))])


def over_basin(values, *before):
    others = [exchange(values, "basin", by) for by in (2, 4, 6)]
    own = after(jnp.stack([values] + others), *before)
    return own, exchange(own, "basin", 1)


def over_basin_in_turn(values, before):
    own = values[None]
    own = after(jnp.concatenate([own, exchange(own, "basin", 2)], axis=0), before)
    own = jnp.concatenate([own, exchange(own, "basin", 4)], axis=0)
    return own, exchange(own, "basin", 1)


def gauge_columns(gauge_reach):
    return jnp.broadcast_to(gauge_reach[:, None], (gauge_reach.shape[0], LANES))


def kernel_tables():
    return [pltpu.SMEM((LEVELS * MAXB,), jnp.int32), pltpu.SMEM((LEVELS,), jnp.int32)]


def by_block(values):
    return values.reshape(-1, 1, BLK)


def sent_paths(days, block_level, part, shape_param, scale_param, down_local, in_slot, sends):
    return call(
        functools.partial(path_kernel, days),
        (
            jax.ShapeDtypeStruct((8, WIDTH), jnp.int32),
            jax.ShapeDtypeStruct((SENDS, 2, KROWS, LANES), F32),
            jax.ShapeDtypeStruct((days + 8, WIDTH), F32),
            jax.ShapeDtypeStruct((block_level.shape[0], 2, 3, KROWS, LANES), F32),
        ),
        [block_level, part],
        [by_block(down_local), by_block(in_slot), by_block(shape_param), by_block(scale_param), sends],
        kernel_tables()
        + [pltpu.VMEM((8, WIDTH), F32), pltpu.VMEM((2, KROWS + days, LANES), F32)],
        1_000_000,
        56 * 1024 * 1024,
    )


def path_adjoints(pieces, gauge_ids, nodes, path_weights):
    shards = len(pieces)
    days = shards * pieces[0].shape[0]
    return call(
        functools.partial(path_adjoint_kernel, shards),
        jax.ShapeDtypeStruct((days, WIDTH), F32),
        [],
        pieces + [gauge_ids, nodes, path_weights],
        [
            pltpu.VMEM((2 * days, pieces[0].shape[1]), BF16),
            pltpu.VMEM((SENDS, 2, days, LANES), F32),
            pltpu.VMEM((2, days + KROWS, LANES), F32),
        ],
        4_000_000_000,
    )


def reach_seeds(pieces, gauge_ids, first, end):
    shards = len(pieces)
    days = sum(piece.shape[0] for piece in pieces)
    return call(
        functools.partial(seed_kernel, shards, first),
        jax.ShapeDtypeStruct((end - first, days, BLK), F32),
        [],
        pieces + [gauge_ids],
        [pltpu.VMEM((2 * days, pieces[0].shape[1]), BF16)],
        3_000_000_000,
    )


def all_reaches(inflow, block_level, part, adjoints, composed, first_seeds, last_seeds, weights, down_local, in_slot):
    own_days = inflow.shape[0]
    blocks, days = block_level.shape[0], first_seeds.shape[1]
    reaches = blocks * BLK
    return call(
        functools.partial(full_kernel, own_days),
        (jax.ShapeDtypeStruct((own_days, reaches), F32), jax.ShapeDtypeStruct((2, reaches), F32)),
        [block_level, part],
        [*adjoints, *composed, first_seeds, last_seeds, weights, inflow, by_block(down_local), by_block(in_slot)],
        kernel_tables()
        + [
            pltpu.VMEM((2 * days, SENDS * WIDTH), BF16),
            pltpu.VMEM((2, days, LANES), F32),
            pltpu.VMEM((2, 2 * days, LANES), F32),
            pltpu.VMEM((2, days + KROWS, LANES), F32),
            pltpu.VMEM((2, 2 * days, MAXB * BLK), BF16),
        ],
        10_000_000_000,
    )


def after(values, *others):
    return lax.optimization_barrier((values, *others))[0]


def fast_shards(
    inflow, cotangent, gauge_reach, shape_param, scale_param, block_level, down_local, in_slot, send_reach,
):
    own_days = inflow.shape[0]
    blocks = block_level.shape[0]
    shards = lax.axis_size("tm")
    days = shards * own_days
    part = lax.axis_index("basin").astype(jnp.int32).reshape(1)
    nodes, path_weights, composed, weights = sent_paths(
        days, block_level, part, shape_param, scale_param, down_local, in_slot, send_reach.reshape(SENDS, 1, KROWS)
    )
    back = lambda by, reach: [(i + by, i) for i in range(shards - reach)]
    following = lax.ppermute(cotangent, "tm", back(1, 1))
    following, composed = lax.optimization_barrier((following, composed, nodes))[:2]
    second = lax.ppermute(following, "tm", back(1, 2))
    third = lax.ppermute(following, "tm", back(2, 3))
    gauge_ids = gauge_columns(gauge_reach)
    composed = over_basin_in_turn(composed, after(second, gauge_ids))
    third, second, nodes, gauge_ids = lax.optimization_barrier((third, second, nodes, gauge_ids))
    pieces = [cotangent, following, second, third]
    adjoints = path_adjoints(pieces, gauge_ids, nodes, path_weights)
    first_seeds = reach_seeds(pieces, gauge_ids, 0, blocks // 2)
    adjoints = over_basin(adjoints, first_seeds)
    last_seeds = reach_seeds(after(pieces, adjoints[0]), gauge_ids, blocks // 2, blocks)
    lateral, params = all_reaches(
        inflow, block_level, part, adjoints, composed, first_seeds, last_seeds, weights, down_local, in_slot
    )
    first, second, third = (exchange(params, "tm", by) for by in (1, 2, 3))
    return lateral, (params + first) + (second + third)


def passed_along(shard, axis, by):
    peers = lax.axis_size(axis)
    pairs = [(i, i + by) for i in range(peers) if 0 <= i + by < peers]
    return lax.ppermute(shard, axis, pairs)


def kernel_of(shape_param, scale_param, lag_count):
    offsets = jnp.arange(lag_count, dtype=jnp.float32) + 0.5
    logits = (shape_param[None, :] - 1.0) * jnp.log(offsets)[:, None] - offsets[
        :, None
    ] / scale_param[None, :]
    weights = jnp.exp(logits)
    return (weights / jnp.sum(weights, axis=0, keepdims=True), offsets)


def lag_adjoint(kernel, extended, day_count):
    summed = kernel[0][None, :] * extended[0:day_count]
    for lag_index in range(1, kernel.shape[0]):
        summed = summed + kernel[lag_index][None, :] * extended[lag_index : lag_index + day_count]
    return summed


def lag_gradient(adjoint_in, inflow_ext, lag_count, day_count):
    per_lag = []
    for lag_index in range(lag_count):
        first_day = lag_count - 1 - lag_index
        per_lag.append(jnp.sum(adjoint_in * inflow_ext[first_day : first_day + day_count], axis=0))
    return jnp.stack(per_lag)


def param_terms(kernel, offsets, scale_param, kernel_grad):
    weighted = jnp.sum(kernel * kernel_grad, axis=0, keepdims=True)
    logit_grad = kernel * (kernel_grad - weighted)
    shape_grad = jnp.sum(logit_grad * jnp.log(offsets)[:, None], axis=0)
    scale_grad = jnp.sum(logit_grad * offsets[:, None], axis=0) / (scale_param * scale_param)
    return jnp.stack([shape_grad, scale_grad])


def take_blocks(values, chosen, block_count):
    rows = values.shape[0]
    picked = jnp.take(values.reshape(rows, block_count, BLK), chosen, axis=1)
    return picked.reshape(rows, chosen.shape[0] * BLK)


def inbound(seed_part, adjoint_all, received, below_reach, slot_of):
    local_part = jnp.where(
        below_reach[None, :] >= 0, adjoint_all[:, jnp.maximum(below_reach, 0)], 0.0
    )
    remote_part = jnp.where(slot_of[None, :] >= 0, received[:, jnp.maximum(slot_of, 0)], 0.0)
    return seed_part + local_part + remote_part


def shards(
    inflow,
    cotangent,
    gauge_reach,
    shape_param,
    scale_param,
    block_level,
    down_local,
    in_slot,
    send_reach,
):
    day_count, reach_count = inflow.shape
    lag_count = LAGS
    block_count = block_level.shape[0]
    kernel, offsets = kernel_of(shape_param, scale_param, lag_count)
    gauge_seed = jnp.zeros((day_count, reach_count), jnp.float32).at[:, gauge_reach].add(cotangent)
    earlier = passed_along(inflow[day_count - (lag_count - 1) :], "tm", 1)
    inflow_ext = jnp.concatenate([earlier, inflow], axis=0)
    adjoint_all = jnp.zeros((day_count, reach_count), jnp.float32)
    kernel_grad = jnp.zeros((lag_count, reach_count), jnp.float32)
    received = jnp.zeros((day_count, send_reach.shape[2]), jnp.float32)
    slot_ids = jnp.arange(MAXB, dtype=jnp.int32)
    block_ids = jnp.arange(block_count, dtype=jnp.int32)
    down_rows = down_local.reshape(1, reach_count)
    slot_rows = in_slot.reshape(1, reach_count)
    for height in range(LEVELS):
        at_height = block_level == height
        rank_of = jnp.cumsum(at_height.astype(jnp.int32)) - 1
        slot_hits = at_height[None, :] & (rank_of[None, :] == slot_ids[:, None])
        slot_valid = jnp.any(slot_hits, axis=1)
        chosen = jnp.sum(jnp.where(slot_hits, block_ids[None, :], 0), axis=1)
        below_reach = take_blocks(down_rows, chosen, block_count)[0]
        slot_of = take_blocks(slot_rows, chosen, block_count)[0]
        seed_part = take_blocks(gauge_seed, chosen, block_count)
        adjoint_in = inbound(seed_part, adjoint_all, received, below_reach, slot_of)
        later_head = passed_along(adjoint_in[: lag_count - 1], "tm", -1)
        extended = jnp.concatenate([adjoint_in, later_head], axis=0)
        outflow = lag_adjoint(take_blocks(kernel, chosen, block_count), extended, day_count)
        lag_grads = lag_gradient(
            adjoint_in, take_blocks(inflow_ext, chosen, block_count), lag_count, day_count
        )
        target_blocks = jnp.where(slot_valid, chosen, block_count)
        adjoint_all = (
            adjoint_all.reshape(day_count, block_count, BLK)
            .at[:, target_blocks]
            .set(outflow.reshape(day_count, MAXB, BLK), mode="drop")
            .reshape(day_count, reach_count)
        )
        kernel_grad = (
            kernel_grad.reshape(lag_count, block_count, BLK)
            .at[:, target_blocks]
            .set(lag_grads.reshape(lag_count, MAXB, BLK), mode="drop")
            .reshape(lag_count, reach_count)
        )
        if height + 1 < LEVELS:
            wanted = send_reach[0, height]
            outgoing = jnp.where(wanted[None, :] >= 0, adjoint_all[:, jnp.maximum(wanted, 0)], 0.0)
            received = lax.all_to_all(outgoing, "basin", split_axis=1, concat_axis=1, tiled=True)
    kernel_total = lax.psum(kernel_grad, "tm")
    param_grad = param_terms(kernel, offsets, scale_param, kernel_total)
    return (adjoint_all, param_grad)


def solution(mesh):
    in_specs = (
        P("tm", "basin"),
        P("tm", "basin"),
        P("basin"),
        P("basin"),
        P("basin"),
        P("basin"),
        P("basin"),
        P("basin"),
        P("basin", None, None),
    )
    out_specs = (P("tm", "basin"), P(None, "basin"))
    small = mesh.shape["basin"] == 8 and mesh.shape["tm"] == 4
    body = fast_shards if small else shards
    return jax.shard_map(body, mesh=mesh, in_specs=in_specs, out_specs=out_specs, check_vma=False)
```

```python
import functools

import jax
import jax.numpy as jnp
from jax import lax
from jax.experimental import pallas as pl
from jax.experimental.pallas import tpu as pltpu
from jax.sharding import PartitionSpec as P

BLK = 256
LAGS = 30
LEVELS = 8
MAXB = 4
LANES = 128
KROWS = 32
SENDS = LEVELS - 1
WIDTH = 2 * LANES
F32 = jnp.float32
BF16 = jnp.bfloat16
VMEM_LIMIT = 20 * 1024 * 1024
JOINT = 4


def iota(shape, axis):
    return lax.broadcasted_iota(jnp.int32, shape, axis)


def split_terms(values):
    high = values.astype(BF16)
    return high, (values - high.astype(F32)).astype(BF16)


def one_hot(hits):
    return jnp.where(hits, 1.0, 0.0).astype(BF16)


def product(left, right):
    return jnp.dot(left, right, preferred_element_type=F32)


def list_blocks(level_ref, order_ref, count_ref):
    for height in range(LEVELS):
        count_ref[height] = 0

    @pl.loop(0, level_ref.shape[0])
    def _(block):
        height = level_ref[block]
        rank = count_ref[height]
        order_ref[height * MAXB + rank] = block
        count_ref[height] = rank + 1


def lag_weights(shape_row, scale_row):
    rows = iota((KROWS, shape_row.shape[1]), 0)
    offsets = rows.astype(F32) + 0.5
    logs = jnp.log(offsets)
    weights = jnp.exp((shape_row - 1.0) * logs - offsets / scale_row)
    weights = jnp.where(rows < LAGS, weights, 0.0)
    return weights / jnp.sum(weights, axis=0, keepdims=True), offsets, logs


def lag_sum(buf, chunk, weight_of, days, lags=LAGS):
    total = jnp.zeros((days, LANES), F32)
    for shift in range(8):
        steps = [k for k in range(shift, lags, 8)]
        shifted = buf[chunk, pl.ds(shift, days + 8 * (len(steps) - 1)), :]
        for step, lag in enumerate(steps):
            total = total + weight_of(lag) * shifted[8 * step : 8 * step + days]
    return total


def lag_sum_forward(buf, chunk, weights_of, days):
    totals = [jnp.zeros((days, LANES), F32) for _ in weights_of]
    for shift in range(8):
        shifted = buf[chunk, pl.ds(8 - shift, days + 24), :]
        for step in range(4):
            lag = 8 * step + shift
            if lag < LAGS:
                part = shifted[24 - 8 * step : 24 - 8 * step + days]
                totals = [t + w(lag) * part for t, w in zip(totals, weights_of)]
    return totals


def fill_weights(shape_ref, scale_ref, weight_ref):
    @pl.loop(0, shape_ref.shape[0])
    def _(block):
        scale_row = scale_ref[block]
        weights, offsets, logs = lag_weights(shape_ref[block], scale_row)
        by_shape = weights * (logs - jnp.sum(weights * logs, axis=0, keepdims=True))
        by_scale = weights * (offsets - jnp.sum(weights * offsets, axis=0, keepdims=True))
        by_scale = by_scale / (scale_row * scale_row)
        for chunk in range(2):
            lanes = slice(chunk * LANES, (chunk + 1) * LANES)
            for which, rows in enumerate((weights, by_shape, by_scale)):
                weight_ref[block, chunk, which] = rows[:, lanes]


def path_kernel(
    days, level_ref, part_ref, down_ref, slot_ref, shape_ref, scale_ref, send_ref, weight_ref,
    comp_ref, reach_weight_ref, order_ref, count_ref, term_ref, buf_ref,
):
    fill_weights(shape_ref, scale_ref, reach_weight_ref)
    list_blocks(level_ref, order_ref, count_ref)
    me = part_ref[0]
    width = WIDTH
    turn = me & 3
    halves = []
    for half in range(2):
        listed = [
            send_ref[h] if h < SENDS else jnp.full((1, KROWS), -1, jnp.int32)
            for h in range(4 * half, 4 * half + 4)
        ]
        listed = jnp.broadcast_to(jnp.concatenate(listed, axis=1), (8, LANES))
        halves.append(pltpu.roll(listed, turn * KROWS, 1)[0:1])
    want = jnp.concatenate(halves, axis=1)
    lane_id = iota((1, width), 1)
    want_level = (lane_id >> 7) * 4 + ((((lane_id & (LANES - 1)) >> 5) - turn) & 3)
    blank = jnp.zeros((4, BLK), F32)
    below = jnp.full((1, width), -1, jnp.int32)
    parent = jnp.full((1, width), -1, jnp.int32)
    rows = iota((BLK, width), 0)
    krows = iota((KROWS, width), 0)
    for height in range(SENDS - 1, -1, -1):
        node = jnp.where((want_level == height) & (want >= 0), want, below)

        def gather(index, total, node=node, height=height):
            block = order_ref[height * MAXB + index]
            hits = one_hot(rows == node - block * BLK)
            table = jnp.concatenate(
                [
                    down_ref[block].astype(F32),
                    slot_ref[block].astype(F32),
                    shape_ref[block],
                    scale_ref[block],
                    blank,
                ],
                axis=0,
            )
            high = table.astype(BF16)
            rest = table - high.astype(F32)
            middle = rest.astype(BF16)
            low = (rest - middle.astype(F32)).astype(BF16)
            return total + product(jnp.concatenate([high, middle, low, high * 0], axis=0), hits)

        found = lax.fori_loop(0, count_ref[height], gather, jnp.zeros((32, width), F32))
        found = (found[0:8] + found[8:16]) + found[16:24]
        active = node >= 0
        down = jnp.round(found[0:1]).astype(jnp.int32)
        slot = jnp.round(found[1:2]).astype(jnp.int32)
        shape_row = jnp.where(active, found[2:3], 2.0)
        scale_row = jnp.where(active, found[3:4], 2.0)
        ends = active & (slot >= 0)
        below = jnp.where(active & (down >= 0), down, -1)
        sender = slot >> 2
        lane = (sender >> 2) * LANES + ((sender + (height - 1)) & 3) * KROWS + me * 4 + (slot & 3)
        parent = jnp.where(ends, (height - 1) * width + lane, parent)
        weights = lag_weights(shape_row, scale_row)[0]
        weights = jnp.where(active, weights, jnp.where(krows == 0, 1.0, 0.0))
        weights = jnp.where(krows == KROWS - 1, node.astype(F32), weights)
        term_ref[height : height + 1, :] = jnp.where(ends, 1.0, 0.0)
        for chunk in range(width // LANES):
            weight_ref[height, chunk] = weights[:, chunk * LANES : (chunk + 1) * LANES]
    buf_ref[...] = jnp.zeros(buf_ref.shape, F32)
    first = iota((8, LANES), 0) == 0
    for height in range(1, SENDS):
        for chunk in range(height // 4, width // LANES):
            ends = term_ref[height : height + 1, chunk * LANES : (chunk + 1) * LANES] > 0.5
            start = buf_ref[chunk, KROWS : KROWS + 8, :]
            buf_ref[chunk, KROWS : KROWS + 8, :] = jnp.where(first & ends, 1.0, start)

        @pl.loop(height // 4, width // LANES)
        def _(chunk, height=height):
            row = lambda lag: weight_ref[height, chunk, pl.ds(lag, 1), :]
            (total,) = lag_sum_forward(buf_ref, chunk, [row], days)
            buf_ref[chunk, KROWS : KROWS + days, :] = total

    for chunk in range(width // LANES):
        lanes = slice(chunk * LANES, (chunk + 1) * LANES)
        comp_ref[0:days, lanes] = buf_ref[chunk, KROWS : KROWS + days, :]
    comp_ref[days : days + 8, :] = jnp.broadcast_to(parent.astype(F32), (8, width))


def grad_kernel(inflow_ref, weight_ref, grad_ref, buf_ref):
    days = inflow_ref.shape[0]
    buf_ref[...] = jnp.zeros(buf_ref.shape, F32)

    @pl.loop(0, weight_ref.shape[0])
    def _(block):
        for chunk in range(2):
            lanes = slice(chunk * LANES, (chunk + 1) * LANES)
            at = pl.ds(pl.multiple_of(block * BLK + chunk * LANES, LANES), LANES)
            buf_ref[chunk, KROWS : KROWS + days, :] = inflow_ref[:, at]
            rows = [
                lambda lag, chunk=chunk, which=which: weight_ref[block, chunk, which, lag : lag + 1, :]
                for which in (1, 2)
            ]
            for which, total in enumerate(lag_sum_forward(buf_ref, chunk, rows, 2 * days)):
                grad_ref[block, which, :, lanes] = total


def gather_terms(pieces, terms_ref):
    days = terms_ref.shape[0] // 2
    start = 0
    for piece in pieces:
        high, low = split_terms(piece[...])
        end = start + piece.shape[0]
        terms_ref[start:end, :] = high
        terms_ref[days + start : days + end, :] = low
        start = end


def gauge_hits(gauge_ref, targets):
    return jnp.concatenate(
        [one_hot(gauge_ref[...] == targets[:, c * LANES : (c + 1) * LANES]) for c in range(2)], axis=1
    )


def folded(total):
    days = total.shape[0] // 2
    return total[:days] + total[days:]


def path_adjoint_kernel(shards, *refs):
    pieces = refs[:shards]
    gauge_ref, weight_ref, out_ref, terms_ref, seed_ref, buf_ref = refs[shards:]
    days = out_ref.shape[0]
    gather_terms(pieces, terms_ref)

    @pl.loop(0, SENDS)
    def _(height):
        nodes = [weight_ref[height, chunk, KROWS - 1 : KROWS, :] for chunk in range(2)]
        nodes = jnp.round(jnp.concatenate(nodes, axis=1)).astype(jnp.int32)
        seeds = folded(product(terms_ref[...], gauge_hits(gauge_ref, nodes)))
        for chunk in range(2):
            seed_ref[height, chunk] = seeds[:, chunk * LANES : (chunk + 1) * LANES]

    for chunk in range(2):
        buf_ref[chunk] = jnp.zeros(buf_ref.shape[1:], F32)

        @pl.loop(0, min(SENDS, 4 * chunk + 4))
        def _(height, chunk=chunk):
            buf_ref[chunk, 0:days, :] = buf_ref[chunk, 0:days, :] + seed_ref[height, chunk]
            row = lambda lag: weight_ref[height, chunk, pl.ds(lag, 1), :]
            buf_ref[chunk, 0:days, :] = lag_sum(buf_ref, chunk, row, days)

        out_ref[:, chunk * LANES : (chunk + 1) * LANES] = buf_ref[chunk, 0:days, :]


def seed_kernel(shards, *refs):
    pieces = refs[:shards]
    row_ref, gauge_ref, out_ref, terms_ref, hits_ref = refs[shards:]
    gather_terms(pieces, terms_ref)
    places = gauge_ref[...] & (BLK - 1)
    for chunk in range(2):
        lanes = iota((1, LANES), 1) + chunk * LANES
        hits_ref[:, chunk * LANES : (chunk + 1) * LANES] = one_hot(places == lanes)
    blocks = row_ref[...] // BLK

    rows = terms_ref.shape[0]

    @pl.loop(0, out_ref.shape[0] // JOINT)
    def _(group):
        masked = [terms_ref[...] * one_hot(blocks == group * JOINT + i) for i in range(JOINT)]
        total = product(jnp.concatenate(masked, axis=0), hits_ref[...])
        for i in range(JOINT):
            out_ref[group * JOINT + i] = folded(total[i * rows : (i + 1) * rows])


def full_kernel(
    own_days, level_ref, part_ref, a_own_ref, a_mate_ref, c_own_ref, c_mate_ref, seed_ref, weight_ref,
    grad_ref, down_ref, slot_ref, out_ref, param_ref,
    order_ref, count_ref, recv_ref, comp_ref, parent_buf, adj_ref, lat_ref,
):
    list_blocks(level_ref, order_ref, count_ref)
    me = part_ref[0]
    flip = (me >> 2) * LANES
    days = seed_ref.shape[1]
    width = 2 * LANES
    groups = iota((1, LANES), 1) >> 5
    rows = iota((BLK, width), 0)

    def merged(own_ref, mate_ref, height, half, at):
        lanes = slice((height // 4) * LANES, (height // 4 + 1) * LANES)
        total = None
        for ref, core in ((own_ref, 0), (mate_ref, 1)):
            for index in (2 * half, 2 * half + 1):
                sender = me ^ (core + 2 * index)
                part = ref[index, at, lanes]
                mine = groups == ((height + sender) & 3)
                total = part if total is None else jnp.where(mine, part, total)
        return total

    def days_of(height):
        return min(days, -(-(own_days + (LAGS - 1) * (LEVELS - 1 - height)) // 16) * 16)

    parent_buf[...] = jnp.zeros(parent_buf.shape, F32)
    for height in range(SENDS):
        if height:
            parents = jnp.concatenate(
                [
                    merged(c_own_ref, c_mate_ref, height, half, slice(days, days + 8))[0:1]
                    for half in range(2)
                ],
                axis=1,
            )
            parents = jnp.round(parents).astype(jnp.int32)
            parents = jnp.where(parents >= 0, parents ^ flip, -1)
            hits = jnp.concatenate(
                [one_hot(rows == parents - lower * width) for lower in range(height)], axis=0
            )
            total = product(recv_ref[:, 0 : height * width], hits)
            total = total[:days] + total[days:]
            for half in range(2):
                parent_buf[half, 0:days, :] = total[:, half * LANES : (half + 1) * LANES]
                comp_ref[half] = merged(c_own_ref, c_mate_ref, height, half, slice(0, days))
        lags = min(days, (LAGS - 1) * height + 1)
        for half in range(2):
            result = merged(a_own_ref, a_mate_ref, height, half, slice(0, days))
            if height:
                count = days_of(height) // 8
                tiles = [result[8 * i : 8 * i + 8] for i in range(days // 8)]
                for shift in range(8):
                    steps = [k for k in range(shift, lags, 8)]
                    for step, lag in enumerate(steps):
                        weight = comp_ref[half, lag : lag + 1, :]
                        for i in range(min(count, days // 8 - step)):
                            at = 8 * (i + step) + shift
                            tiles[i] = tiles[i] + weight * parent_buf[half, at : at + 8, :]
                result = jnp.concatenate(tiles, axis=0)
            high, low = split_terms(result)
            lanes = slice(height * width + half * LANES, height * width + (half + 1) * LANES)
            recv_ref[0:days, lanes] = high
            recv_ref[days : 2 * days, lanes] = low

    adj_ref[...] = jnp.zeros(adj_ref.shape, F32)
    lat_ref[...] = jnp.zeros(lat_ref.shape, BF16)

    def level(height, sources):
        need = days_of(height)
        have = days_of(height - 1) if height else days
        count = count_ref[height]

        def gather(rank):
            block = order_ref[height * MAXB + rank]
            seeds = seed_ref[block, 0:have, :]
            if not height:
                return seeds
            slot = slot_ref[block]
            sender = slot >> 2
            lane = ((sender >> 2) * LANES ^ flip) + ((sender + (height - 1)) & 3) * KROWS
            lane = jnp.where(slot >= 0, lane + me * 4 + (slot & 3), -1)
            down = down_ref[block]
            hits = [one_hot(rows == lane)]
            for index in range(sources):
                source = jnp.where(
                    index < count_ref[height - 1], order_ref[(height - 1) * MAXB + index], -2
                )
                hits.append(one_hot((rows == down - source * BLK) & (down >= 0)))
            terms = []
            for start, first in ((0, 0), (have, days)):
                local = lat_ref[(height - 1) % 2, start : start + have, 0 : sources * BLK]
                received = recv_ref[first : first + have, (height - 1) * width : height * width]
                terms.append(jnp.concatenate([received, local], axis=1))
            total = product(jnp.concatenate(terms, axis=0), jnp.concatenate(hits, axis=0))
            return seeds + total[:have] + total[have:]

        @pl.loop(0, count)
        def _(rank):
            adjoint = gather(rank)
            block = order_ref[height * MAXB + rank]
            for chunk in range(2):
                lanes = slice(chunk * LANES, (chunk + 1) * LANES)
                adj_ref[chunk, 0:have, :] = adjoint[:, lanes]
                at = pl.ds(pl.multiple_of(block * BLK + chunk * LANES, LANES), LANES)
                for which in range(2):
                    grads = adjoint[: 2 * own_days, lanes] * grad_ref[block, which, :, lanes]
                    param_ref[which : which + 1, at] = jnp.sum(grads, axis=0, keepdims=True)
                row = lambda lag, chunk=chunk: weight_ref[block, chunk, 0, lag : lag + 1, :]
                result = lag_sum(adj_ref, chunk, row, need)
                out_ref[:, at] = result[:own_days]
                if height + 1 < LEVELS:
                    high, low = split_terms(result)
                    lanes = pl.ds(pl.multiple_of(rank * BLK + chunk * LANES, LANES), LANES)
                    lat_ref[height % 2, 0:need, lanes] = high
                    lat_ref[height % 2, need : 2 * need, lanes] = low

    level(0, 0)
    for height in range(1, LEVELS):
        few = count_ref[height - 1] <= MAXB // 2
        pl.when(few)(functools.partial(level, height, MAXB // 2))
        pl.when(jnp.logical_not(few))(functools.partial(level, height, MAXB))


def call(kernel, out_shape, in_smem, in_vmem, scratch, flops, limit=VMEM_LIMIT):
    vmem = pl.BlockSpec(memory_space=pltpu.VMEM)
    smem = pl.BlockSpec(memory_space=pltpu.SMEM)
    return pl.pallas_call(
        kernel,
        out_shape=out_shape,
        in_specs=[smem] * len(in_smem) + [vmem] * len(in_vmem),
        out_specs=jax.tree.map(lambda _: vmem, out_shape),
        scratch_shapes=scratch,
        compiler_params=pltpu.CompilerParams(vmem_limit_bytes=limit),
        cost_estimate=pl.CostEstimate(
            flops=flops,
            bytes_accessed=flops // 1000,
            transcendentals=0,
        ),
    )(*in_smem, *in_vmem)


def exchange(values, axis, by):
    return lax.ppermute(values, axis, [(i, i ^ by) for i in range(lax.axis_size(axis))])


def over_basin(values, *before):
    others = [exchange(values, "basin", by) for by in (2, 4, 6)]
    own = after(jnp.stack([values] + others), *before)
    return own, exchange(own, "basin", 1)


def gauge_columns(gauge_reach):
    return jnp.broadcast_to(gauge_reach[:, None], (gauge_reach.shape[0], LANES))


def kernel_tables():
    return [pltpu.SMEM((LEVELS * MAXB,), jnp.int32), pltpu.SMEM((LEVELS,), jnp.int32)]


def by_block(values):
    return values.reshape(-1, 1, BLK)


def sent_paths(days, block_level, part, shape_param, scale_param, down_local, in_slot, sends):
    return call(
        functools.partial(path_kernel, days),
        (
            jax.ShapeDtypeStruct((SENDS, 2, KROWS, LANES), F32),
            jax.ShapeDtypeStruct((days + 8, WIDTH), F32),
            jax.ShapeDtypeStruct((block_level.shape[0], 2, 3, KROWS, LANES), F32),
        ),
        [block_level, part],
        [by_block(down_local), by_block(in_slot), by_block(shape_param), by_block(scale_param), sends],
        kernel_tables()
        + [pltpu.VMEM((8, WIDTH), F32), pltpu.VMEM((2, KROWS + days, LANES), F32)],
        1_000_000,
        56 * 1024 * 1024,
    )


def path_adjoints(pieces, gauge_ids, path_weights):
    shards = len(pieces)
    days = sum(piece.shape[0] for piece in pieces)
    return call(
        functools.partial(path_adjoint_kernel, shards),
        jax.ShapeDtypeStruct((days, WIDTH), F32),
        [],
        pieces + [gauge_ids, path_weights],
        [
            pltpu.VMEM((2 * days, pieces[0].shape[1]), BF16),
            pltpu.VMEM((SENDS, 2, days, LANES), F32),
            pltpu.VMEM((2, days + KROWS, LANES), F32),
        ],
        4_000_000_000,
    )


def reach_seeds(pieces, gauge_reach, gauge_ids, blocks):
    shards = len(pieces)
    days = sum(piece.shape[0] for piece in pieces)
    gauges = gauge_reach.shape[0]
    return call(
        functools.partial(seed_kernel, shards),
        jax.ShapeDtypeStruct((blocks, days, BLK), F32),
        [],
        pieces + [gauge_reach.reshape(1, gauges), gauge_ids],
        [pltpu.VMEM((2 * days, gauges), BF16), pltpu.VMEM((gauges, BLK), BF16)],
        3_000_000_000,
    )


def day_grads(inflow, weights):
    own_days = inflow.shape[0]
    return call(
        grad_kernel,
        jax.ShapeDtypeStruct((weights.shape[0], 2, 2 * own_days, BLK), F32),
        [],
        [inflow, weights],
        [pltpu.VMEM((2, KROWS + 2 * own_days, LANES), F32)],
        1_000_000,
    )


def all_reaches(block_level, part, adjoints, composed, seeds, weights, grads, down_local, in_slot):
    own_days = grads.shape[2] // 2
    blocks, days = block_level.shape[0], seeds.shape[1]
    reaches = blocks * BLK
    return call(
        functools.partial(full_kernel, own_days),
        (jax.ShapeDtypeStruct((own_days, reaches), F32), jax.ShapeDtypeStruct((2, reaches), F32)),
        [block_level, part],
        [*adjoints, *composed, seeds, weights, grads, by_block(down_local), by_block(in_slot)],
        kernel_tables()
        + [
            pltpu.VMEM((2 * days, SENDS * WIDTH), BF16),
            pltpu.VMEM((2, days, LANES), F32),
            pltpu.VMEM((2, 2 * days, LANES), F32),
            pltpu.VMEM((2, days + KROWS, LANES), F32),
            pltpu.VMEM((2, 2 * days, MAXB * BLK), BF16),
        ],
        10_000_000_000,
    )


def after(values, *others):
    return lax.optimization_barrier((values, *others))[0]


def fast_shards(
    inflow, cotangent, gauge_reach, shape_param, scale_param, block_level, down_local, in_slot, send_reach,
):
    own_days = inflow.shape[0]
    blocks = block_level.shape[0]
    shards = lax.axis_size("tm")
    days = shards * own_days
    gauge_ids = gauge_columns(gauge_reach)
    part = after(lax.axis_index("basin").astype(jnp.int32).reshape(1), gauge_ids)
    path_weights, composed, weights = sent_paths(
        days, block_level, part, shape_param, scale_param, down_local, in_slot, send_reach.reshape(SENDS, 1, KROWS)
    )
    back = lambda by, reach: [(i + by, i) for i in range(shards - reach)]
    following = lax.ppermute(cotangent, "tm", back(1, 1))
    following, composed, path_weights = lax.optimization_barrier((following, composed, path_weights))
    second = lax.ppermute(following, "tm", back(1, 2))
    third = lax.ppermute(following, "tm", back(2, 3))
    early = jnp.concatenate([cotangent, following], axis=0)
    path_weights = jnp.pad(path_weights, ((0, 1), (0, 0), (0, 0), (0, 0)))
    composed = jnp.concatenate([composed[None], exchange(composed[None], "basin", 2)], axis=0)
    composed, early, path_weights, weights = lax.optimization_barrier(
        (composed, early, path_weights, weights)
    )
    grads = day_grads(inflow, weights)
    composed = jnp.concatenate([composed, exchange(composed, "basin", 4)], axis=0)
    composed = (composed, exchange(composed, "basin", 1))
    third, second, grads = lax.optimization_barrier((third, second, grads))
    pieces = [early, second, third]
    adjoints = path_adjoints(pieces, gauge_ids, path_weights)
    seeds = reach_seeds(pieces, gauge_reach, gauge_ids, blocks)
    adjoints = over_basin(adjoints, seeds)
    lateral, params = all_reaches(
        block_level, part, adjoints, composed, seeds, weights, grads, down_local, in_slot
    )
    first, second, third = (exchange(params, "tm", by) for by in (1, 2, 3))
    return lateral, (params + first) + (second + third)


def passed_along(shard, axis, by):
    peers = lax.axis_size(axis)
    pairs = [(i, i + by) for i in range(peers) if 0 <= i + by < peers]
    return lax.ppermute(shard, axis, pairs)


def kernel_of(shape_param, scale_param, lag_count):
    offsets = jnp.arange(lag_count, dtype=jnp.float32) + 0.5
    logits = (shape_param[None, :] - 1.0) * jnp.log(offsets)[:, None] - offsets[
        :, None
    ] / scale_param[None, :]
    weights = jnp.exp(logits)
    return (weights / jnp.sum(weights, axis=0, keepdims=True), offsets)


def lag_adjoint(kernel, extended, day_count):
    summed = kernel[0][None, :] * extended[0:day_count]
    for lag_index in range(1, kernel.shape[0]):
        summed = summed + kernel[lag_index][None, :] * extended[lag_index : lag_index + day_count]
    return summed


def lag_gradient(adjoint_in, inflow_ext, lag_count, day_count):
    per_lag = []
    for lag_index in range(lag_count):
        first_day = lag_count - 1 - lag_index
        per_lag.append(jnp.sum(adjoint_in * inflow_ext[first_day : first_day + day_count], axis=0))
    return jnp.stack(per_lag)


def param_terms(kernel, offsets, scale_param, kernel_grad):
    weighted = jnp.sum(kernel * kernel_grad, axis=0, keepdims=True)
    logit_grad = kernel * (kernel_grad - weighted)
    shape_grad = jnp.sum(logit_grad * jnp.log(offsets)[:, None], axis=0)
    scale_grad = jnp.sum(logit_grad * offsets[:, None], axis=0) / (scale_param * scale_param)
    return jnp.stack([shape_grad, scale_grad])


def take_blocks(values, chosen, block_count):
    rows = values.shape[0]
    picked = jnp.take(values.reshape(rows, block_count, BLK), chosen, axis=1)
    return picked.reshape(rows, chosen.shape[0] * BLK)


def inbound(seed_part, adjoint_all, received, below_reach, slot_of):
    local_part = jnp.where(
        below_reach[None, :] >= 0, adjoint_all[:, jnp.maximum(below_reach, 0)], 0.0
    )
    remote_part = jnp.where(slot_of[None, :] >= 0, received[:, jnp.maximum(slot_of, 0)], 0.0)
    return seed_part + local_part + remote_part


def shards(
    inflow,
    cotangent,
    gauge_reach,
    shape_param,
    scale_param,
    block_level,
    down_local,
    in_slot,
    send_reach,
):
    day_count, reach_count = inflow.shape
    lag_count = LAGS
    block_count = block_level.shape[0]
    kernel, offsets = kernel_of(shape_param, scale_param, lag_count)
    gauge_seed = jnp.zeros((day_count, reach_count), jnp.float32).at[:, gauge_reach].add(cotangent)
    earlier = passed_along(inflow[day_count - (lag_count - 1) :], "tm", 1)
    inflow_ext = jnp.concatenate([earlier, inflow], axis=0)
    adjoint_all = jnp.zeros((day_count, reach_count), jnp.float32)
    kernel_grad = jnp.zeros((lag_count, reach_count), jnp.float32)
    received = jnp.zeros((day_count, send_reach.shape[2]), jnp.float32)
    slot_ids = jnp.arange(MAXB, dtype=jnp.int32)
    block_ids = jnp.arange(block_count, dtype=jnp.int32)
    down_rows = down_local.reshape(1, reach_count)
    slot_rows = in_slot.reshape(1, reach_count)
    for height in range(LEVELS):
        at_height = block_level == height
        rank_of = jnp.cumsum(at_height.astype(jnp.int32)) - 1
        slot_hits = at_height[None, :] & (rank_of[None, :] == slot_ids[:, None])
        slot_valid = jnp.any(slot_hits, axis=1)
        chosen = jnp.sum(jnp.where(slot_hits, block_ids[None, :], 0), axis=1)
        below_reach = take_blocks(down_rows, chosen, block_count)[0]
        slot_of = take_blocks(slot_rows, chosen, block_count)[0]
        seed_part = take_blocks(gauge_seed, chosen, block_count)
        adjoint_in = inbound(seed_part, adjoint_all, received, below_reach, slot_of)
        later_head = passed_along(adjoint_in[: lag_count - 1], "tm", -1)
        extended = jnp.concatenate([adjoint_in, later_head], axis=0)
        outflow = lag_adjoint(take_blocks(kernel, chosen, block_count), extended, day_count)
        lag_grads = lag_gradient(
            adjoint_in, take_blocks(inflow_ext, chosen, block_count), lag_count, day_count
        )
        target_blocks = jnp.where(slot_valid, chosen, block_count)
        adjoint_all = (
            adjoint_all.reshape(day_count, block_count, BLK)
            .at[:, target_blocks]
            .set(outflow.reshape(day_count, MAXB, BLK), mode="drop")
            .reshape(day_count, reach_count)
        )
        kernel_grad = (
            kernel_grad.reshape(lag_count, block_count, BLK)
            .at[:, target_blocks]
            .set(lag_grads.reshape(lag_count, MAXB, BLK), mode="drop")
            .reshape(lag_count, reach_count)
        )
        if height + 1 < LEVELS:
            wanted = send_reach[0, height]
            outgoing = jnp.where(wanted[None, :] >= 0, adjoint_all[:, jnp.maximum(wanted, 0)], 0.0)
            received = lax.all_to_all(outgoing, "basin", split_axis=1, concat_axis=1, tiled=True)
    kernel_total = lax.psum(kernel_grad, "tm")
    param_grad = param_terms(kernel, offsets, scale_param, kernel_total)
    return (adjoint_all, param_grad)


def solution(mesh):
    in_specs = (
        P("tm", "basin"),
        P("tm", "basin"),
        P("basin"),
        P("basin"),
        P("basin"),
        P("basin"),
        P("basin"),
        P("basin"),
        P("basin", None, None),
    )
    out_specs = (P("tm", "basin"), P(None, "basin"))
    small = mesh.shape["basin"] == 8 and mesh.shape["tm"] == 4
    body = fast_shards if small else shards
    return jax.shard_map(body, mesh=mesh, in_specs=in_specs, out_specs=out_specs, check_vma=False)
```

```python
import functools

import jax
import jax.numpy as jnp
from jax import lax
from jax.experimental import pallas as pl
from jax.experimental.pallas import tpu as pltpu
from jax.sharding import PartitionSpec as P

BLK = 256
LAGS = 30
LEVELS = 8
MAXB = 4
LANES = 128
KROWS = 32
SENDS = LEVELS - 1
WIDTH = 2 * LANES
F32 = jnp.float32
BF16 = jnp.bfloat16
VMEM_LIMIT = 20 * 1024 * 1024
JOINT = 4


def iota(shape, axis):
    return lax.broadcasted_iota(jnp.int32, shape, axis)


def split_terms(values):
    high = values.astype(BF16)
    return high, (values - high.astype(F32)).astype(BF16)


def one_hot(hits):
    return jnp.where(hits, 1.0, 0.0).astype(BF16)


def product(left, right):
    return jnp.dot(left, right, preferred_element_type=F32)


def list_blocks(level_ref, order_ref, count_ref):
    for height in range(LEVELS):
        count_ref[height] = 0

    @pl.loop(0, level_ref.shape[0])
    def _(block):
        height = level_ref[block]
        rank = count_ref[height]
        order_ref[height * MAXB + rank] = block
        count_ref[height] = rank + 1


def lag_weights(shape_row, scale_row):
    rows = iota((KROWS, shape_row.shape[1]), 0)
    offsets = rows.astype(F32) + 0.5
    logs = jnp.log(offsets)
    weights = jnp.exp((shape_row - 1.0) * logs - offsets / scale_row)
    weights = jnp.where(rows < LAGS, weights, 0.0)
    return weights / jnp.sum(weights, axis=0, keepdims=True), offsets, logs


def lag_sum(buf, chunk, weight_of, days, lags=LAGS):
    total = jnp.zeros((days, LANES), F32)
    for shift in range(8):
        steps = [k for k in range(shift, lags, 8)]
        shifted = buf[chunk, pl.ds(shift, days + 8 * (len(steps) - 1)), :]
        for step, lag in enumerate(steps):
            total = total + weight_of(lag) * shifted[8 * step : 8 * step + days]
    return total


def lag_sum_forward(buf, chunk, weights_of, days):
    totals = [jnp.zeros((days, LANES), F32) for _ in weights_of]
    for shift in range(8):
        shifted = buf[chunk, pl.ds(8 - shift, days + 24), :]
        for step in range(4):
            lag = 8 * step + shift
            if lag < LAGS:
                part = shifted[24 - 8 * step : 24 - 8 * step + days]
                totals = [t + w(lag) * part for t, w in zip(totals, weights_of)]
    return totals


def path_kernel(
    level_ref, part_ref, down_ref, slot_ref, shape_ref, scale_ref, send_ref, weight_ref,
    ends_ref, order_ref, count_ref,
):
    list_blocks(level_ref, order_ref, count_ref)
    me = part_ref[0]
    width = WIDTH
    turn = me & 3
    halves = []
    for half in range(2):
        listed = [
            send_ref[h] if h < SENDS else jnp.full((1, KROWS), -1, jnp.int32)
            for h in range(4 * half, 4 * half + 4)
        ]
        listed = jnp.broadcast_to(jnp.concatenate(listed, axis=1), (8, LANES))
        halves.append(pltpu.roll(listed, turn * KROWS, 1)[0:1])
    want = jnp.concatenate(halves, axis=1)
    lane_id = iota((1, width), 1)
    want_level = (lane_id >> 7) * 4 + ((((lane_id & (LANES - 1)) >> 5) - turn) & 3)
    blank = jnp.zeros((4, BLK), F32)
    below = jnp.full((1, width), -1, jnp.int32)
    parent = jnp.full((1, width), -1, jnp.int32)
    rows = iota((BLK, width), 0)
    krows = iota((KROWS, width), 0)
    for height in range(SENDS - 1, -1, -1):
        node = jnp.where((want_level == height) & (want >= 0), want, below)

        def gather(index, total, node=node, height=height):
            block = order_ref[height * MAXB + index]
            hits = one_hot(rows == node - block * BLK)
            table = jnp.concatenate(
                [
                    down_ref[block].astype(F32),
                    slot_ref[block].astype(F32),
                    shape_ref[block],
                    scale_ref[block],
                    blank,
                ],
                axis=0,
            )
            high = table.astype(BF16)
            rest = table - high.astype(F32)
            middle = rest.astype(BF16)
            low = (rest - middle.astype(F32)).astype(BF16)
            return total + product(jnp.concatenate([high, middle, low, high * 0], axis=0), hits)

        found = lax.fori_loop(0, count_ref[height], gather, jnp.zeros((32, width), F32))
        found = (found[0:8] + found[8:16]) + found[16:24]
        active = node >= 0
        down = jnp.round(found[0:1]).astype(jnp.int32)
        slot = jnp.round(found[1:2]).astype(jnp.int32)
        shape_row = jnp.where(active, found[2:3], 2.0)
        scale_row = jnp.where(active, found[3:4], 2.0)
        ends = active & (slot >= 0)
        below = jnp.where(active & (down >= 0), down, -1)
        sender = slot >> 2
        lane = (sender >> 2) * LANES + ((sender + (height - 1)) & 3) * KROWS + me * 4 + (slot & 3)
        parent = jnp.where(ends, (height - 1) * width + lane, parent)
        weights = lag_weights(shape_row, scale_row)[0]
        weights = jnp.where(active, weights, jnp.where(krows == 0, 1.0, 0.0))
        weights = jnp.where(krows == KROWS - 1, node.astype(F32), weights)
        ends_ref[height : height + 1, :] = jnp.where(ends, 1.0, 0.0)
        for chunk in range(width // LANES):
            weight_ref[height, chunk] = weights[:, chunk * LANES : (chunk + 1) * LANES]
    ends_ref[SENDS : SENDS + 1, :] = parent.astype(F32)


def compose_kernel(ends_ref, weight_ref, comp_ref, buf_ref):
    width = ends_ref.shape[1]
    days = buf_ref.shape[1] - KROWS
    buf_ref[...] = jnp.zeros(buf_ref.shape, F32)
    first = iota((8, LANES), 0) == 0
    for height in range(1, SENDS):
        for chunk in range(height // 4, width // LANES):
            ends = ends_ref[height : height + 1, chunk * LANES : (chunk + 1) * LANES] > 0.5
            start = buf_ref[chunk, KROWS : KROWS + 8, :]
            buf_ref[chunk, KROWS : KROWS + 8, :] = jnp.where(first & ends, 1.0, start)

        @pl.loop(height // 4, width // LANES)
        def _(chunk, height=height):
            row = lambda lag: weight_ref[height, chunk, pl.ds(lag, 1), :]
            (total,) = lag_sum_forward(buf_ref, chunk, [row], days)
            buf_ref[chunk, KROWS : KROWS + days, :] = total

    for chunk in range(width // LANES):
        lanes = slice(chunk * LANES, (chunk + 1) * LANES)
        comp_ref[0:days, lanes] = buf_ref[chunk, KROWS : KROWS + days, :]
    comp_ref[days : days + 8, :] = jnp.broadcast_to(ends_ref[SENDS : SENDS + 1, :], (8, width))


def grad_kernel(inflow_ref, shape_ref, scale_ref, weight_ref, grad_ref, buf_ref, row_ref):
    days = inflow_ref.shape[0]
    buf_ref[...] = jnp.zeros(buf_ref.shape, F32)

    @pl.loop(0, weight_ref.shape[0])
    def _(block):
        scale_row = scale_ref[block]
        weights, offsets, logs = lag_weights(shape_ref[block], scale_row)
        by_shape = weights * (logs - jnp.sum(weights * logs, axis=0, keepdims=True))
        by_scale = weights * (offsets - jnp.sum(weights * offsets, axis=0, keepdims=True))
        by_scale = by_scale / (scale_row * scale_row)
        for chunk in range(2):
            lanes = slice(chunk * LANES, (chunk + 1) * LANES)
            weight_ref[block, chunk] = weights[:, lanes]
            row_ref[chunk, 0] = by_shape[:, lanes]
            row_ref[chunk, 1] = by_scale[:, lanes]
            at = pl.ds(pl.multiple_of(block * BLK + chunk * LANES, LANES), LANES)
            buf_ref[chunk, 8 : 8 + days, :] = inflow_ref[:, at]
        for chunk in range(2):
            lanes = slice(chunk * LANES, (chunk + 1) * LANES)
            totals = [[jnp.zeros((8, LANES), F32) for _ in range(days // 4)] for _ in range(2)]
            for shift in range(8):
                shifted = buf_ref[chunk, pl.ds(8 - shift, days + 8), :]
                for lag in range(shift, LAGS, 8):
                    for which, tiles in enumerate(totals):
                        weight = row_ref[chunk, which, lag : lag + 1, :]
                        for tile in range(days // 8 + 1):
                            at = tile + lag // 8
                            tiles[at] = tiles[at] + weight * shifted[8 * tile : 8 * tile + 8]
            for which, tiles in enumerate(totals):
                grad_ref[block, which, :, lanes] = jnp.concatenate(tiles, axis=0)


def gather_terms(pieces, terms_ref):
    days = terms_ref.shape[0] // 2
    start = 0
    for piece in pieces:
        high, low = split_terms(piece[...])
        end = start + piece.shape[0]
        terms_ref[start:end, :] = high
        terms_ref[days + start : days + end, :] = low
        start = end


def gauge_hits(gauge_ref, targets):
    return jnp.concatenate(
        [one_hot(gauge_ref[...] == targets[:, c * LANES : (c + 1) * LANES]) for c in range(2)], axis=1
    )


def folded(total):
    days = total.shape[0] // 2
    return total[:days] + total[days:]


def path_adjoint_kernel(shards, *refs):
    pieces = refs[:shards]
    gauge_ref, weight_ref, out_ref, terms_ref, seed_ref, buf_ref = refs[shards:]
    days = out_ref.shape[0]
    gather_terms(pieces, terms_ref)

    @pl.loop(0, SENDS)
    def _(height):
        nodes = [weight_ref[height, chunk, KROWS - 1 : KROWS, :] for chunk in range(2)]
        nodes = jnp.round(jnp.concatenate(nodes, axis=1)).astype(jnp.int32)
        seeds = folded(product(terms_ref[...], gauge_hits(gauge_ref, nodes)))
        for chunk in range(2):
            seed_ref[height, chunk] = seeds[:, chunk * LANES : (chunk + 1) * LANES]

    for chunk in range(2):
        buf_ref[chunk] = jnp.zeros(buf_ref.shape[1:], F32)

        @pl.loop(0, min(SENDS, 4 * chunk + 4))
        def _(height, chunk=chunk):
            buf_ref[chunk, 0:days, :] = buf_ref[chunk, 0:days, :] + seed_ref[height, chunk]
            row = lambda lag: weight_ref[height, chunk, pl.ds(lag, 1), :]
            buf_ref[chunk, 0:days, :] = lag_sum(buf_ref, chunk, row, days)

        out_ref[:, chunk * LANES : (chunk + 1) * LANES] = buf_ref[chunk, 0:days, :]


def seed_kernel(shards, *refs):
    pieces = refs[:shards]
    row_ref, gauge_ref, out_ref, terms_ref, hits_ref = refs[shards:]
    gather_terms(pieces, terms_ref)
    places = gauge_ref[...] & (BLK - 1)
    for chunk in range(2):
        lanes = iota((1, LANES), 1) + chunk * LANES
        hits_ref[:, chunk * LANES : (chunk + 1) * LANES] = one_hot(places == lanes)
    blocks = row_ref[...] // BLK

    rows = terms_ref.shape[0]

    @pl.loop(0, out_ref.shape[0] // JOINT)
    def _(group):
        masked = [terms_ref[...] * one_hot(blocks == group * JOINT + i) for i in range(JOINT)]
        total = product(jnp.concatenate(masked, axis=0), hits_ref[...])
        for i in range(JOINT):
            out_ref[group * JOINT + i] = folded(total[i * rows : (i + 1) * rows])


def full_kernel(
    own_days, level_ref, part_ref, a_own_ref, a_mate_ref, c_own_ref, c_mate_ref, seed_ref, weight_ref,
    grad_ref, down_ref, slot_ref, out_ref, param_ref,
    order_ref, count_ref, recv_ref, comp_ref, parent_buf, adj_ref, lat_ref,
):
    list_blocks(level_ref, order_ref, count_ref)
    me = part_ref[0]
    flip = (me >> 2) * LANES
    days = seed_ref.shape[1]
    width = 2 * LANES
    groups = iota((1, LANES), 1) >> 5
    rows = iota((BLK, width), 0)

    def merged(own_ref, mate_ref, height, half, at):
        lanes = slice((height // 4) * LANES, (height // 4 + 1) * LANES)
        total = None
        for ref, core in ((own_ref, 0), (mate_ref, 1)):
            for index in (2 * half, 2 * half + 1):
                sender = me ^ (core + 2 * index)
                part = ref[index, at, lanes]
                mine = groups == ((height + sender) & 3)
                total = part if total is None else jnp.where(mine, part, total)
        return total

    def days_of(height):
        return min(days, -(-(own_days + (LAGS - 1) * (LEVELS - 1 - height)) // 16) * 16)

    parent_buf[...] = jnp.zeros(parent_buf.shape, F32)
    for height in range(SENDS):
        if height:
            parents = jnp.concatenate(
                [
                    merged(c_own_ref, c_mate_ref, height, half, slice(days, days + 8))[0:1]
                    for half in range(2)
                ],
                axis=1,
            )
            parents = jnp.round(parents).astype(jnp.int32)
            parents = jnp.where(parents >= 0, parents ^ flip, -1)
            hits = jnp.concatenate(
                [one_hot(rows == parents - lower * width) for lower in range(height)], axis=0
            )
            total = product(recv_ref[:, 0 : height * width], hits)
            total = total[:days] + total[days:]
            for half in range(2):
                parent_buf[half, 0:days, :] = total[:, half * LANES : (half + 1) * LANES]
                comp_ref[half] = merged(c_own_ref, c_mate_ref, height, half, slice(0, days))
        lags = min(days, (LAGS - 1) * height + 1)
        for half in range(2):
            result = merged(a_own_ref, a_mate_ref, height, half, slice(0, days))
            if height:
                count = days_of(height) // 8
                tiles = [result[8 * i : 8 * i + 8] for i in range(days // 8)]
                for shift in range(8):
                    steps = [k for k in range(shift, lags, 8)]
                    for step, lag in enumerate(steps):
                        weight = comp_ref[half, lag : lag + 1, :]
                        for i in range(min(count, days // 8 - step)):
                            at = 8 * (i + step) + shift
                            tiles[i] = tiles[i] + weight * parent_buf[half, at : at + 8, :]
                result = jnp.concatenate(tiles, axis=0)
            high, low = split_terms(result)
            lanes = slice(height * width + half * LANES, height * width + (half + 1) * LANES)
            recv_ref[0:days, lanes] = high
            recv_ref[days : 2 * days, lanes] = low

    adj_ref[...] = jnp.zeros(adj_ref.shape, F32)
    lat_ref[...] = jnp.zeros(lat_ref.shape, BF16)

    def level(height, sources):
        need = days_of(height)
        have = days_of(height - 1) if height else days
        count = count_ref[height]

        def gather(rank):
            block = order_ref[height * MAXB + rank]
            seeds = seed_ref[block, 0:have, :]
            if not height:
                return seeds
            slot = slot_ref[block]
            sender = slot >> 2
            lane = ((sender >> 2) * LANES ^ flip) + ((sender + (height - 1)) & 3) * KROWS
            lane = jnp.where(slot >= 0, lane + me * 4 + (slot & 3), -1)
            down = down_ref[block]
            hits = [one_hot(rows == lane)]
            for index in range(sources):
                source = jnp.where(
                    index < count_ref[height - 1], order_ref[(height - 1) * MAXB + index], -2
                )
                hits.append(one_hot((rows == down - source * BLK) & (down >= 0)))
            terms = []
            for start, first in ((0, 0), (have, days)):
                local = lat_ref[(height - 1) % 2, start : start + have, 0 : sources * BLK]
                received = recv_ref[first : first + have, (height - 1) * width : height * width]
                terms.append(jnp.concatenate([received, local], axis=1))
            total = product(jnp.concatenate(terms, axis=0), jnp.concatenate(hits, axis=0))
            return seeds + total[:have] + total[have:]

        @pl.loop(0, count)
        def _(rank):
            adjoint = gather(rank)
            block = order_ref[height * MAXB + rank]
            for chunk in range(2):
                lanes = slice(chunk * LANES, (chunk + 1) * LANES)
                adj_ref[chunk, 0:have, :] = adjoint[:, lanes]
                at = pl.ds(pl.multiple_of(block * BLK + chunk * LANES, LANES), LANES)
                for which in range(2):
                    grads = adjoint[: 2 * own_days, lanes] * grad_ref[block, which, :, lanes]
                    param_ref[which : which + 1, at] = jnp.sum(grads, axis=0, keepdims=True)
                row = lambda lag, chunk=chunk: weight_ref[block, chunk, lag : lag + 1, :]
                result = lag_sum(adj_ref, chunk, row, need)
                out_ref[:, at] = result[:own_days]
                if height + 1 < LEVELS:
                    high, low = split_terms(result)
                    lanes = pl.ds(pl.multiple_of(rank * BLK + chunk * LANES, LANES), LANES)
                    lat_ref[height % 2, 0:need, lanes] = high
                    lat_ref[height % 2, need : 2 * need, lanes] = low

    level(0, 0)
    for height in range(1, LEVELS):
        few = count_ref[height - 1] <= MAXB // 2
        pl.when(few)(functools.partial(level, height, MAXB // 2))
        pl.when(jnp.logical_not(few))(functools.partial(level, height, MAXB))


def call(kernel, out_shape, in_smem, in_vmem, scratch, flops, limit=VMEM_LIMIT):
    vmem = pl.BlockSpec(memory_space=pltpu.VMEM)
    smem = pl.BlockSpec(memory_space=pltpu.SMEM)
    return pl.pallas_call(
        kernel,
        out_shape=out_shape,
        in_specs=[smem] * len(in_smem) + [vmem] * len(in_vmem),
        out_specs=jax.tree.map(lambda _: vmem, out_shape),
        scratch_shapes=scratch,
        compiler_params=pltpu.CompilerParams(vmem_limit_bytes=limit),
        cost_estimate=pl.CostEstimate(
            flops=flops,
            bytes_accessed=flops // 1000,
            transcendentals=0,
        ),
    )(*in_smem, *in_vmem)


def exchange(values, axis, by):
    return lax.ppermute(values, axis, [(i, i ^ by) for i in range(lax.axis_size(axis))])


def over_basin(values, *before):
    others = [exchange(values, "basin", by) for by in (2, 4, 6)]
    own = after(jnp.stack([values] + others), *before)
    return own, exchange(own, "basin", 1)


def gauge_columns(gauge_reach):
    return jnp.broadcast_to(gauge_reach[:, None], (gauge_reach.shape[0], LANES))


def kernel_tables():
    return [pltpu.SMEM((LEVELS * MAXB,), jnp.int32), pltpu.SMEM((LEVELS,), jnp.int32)]


def by_block(values):
    return values.reshape(-1, 1, BLK)


def sent_paths(block_level, part, shape_param, scale_param, down_local, in_slot, sends):
    return call(
        path_kernel,
        (
            jax.ShapeDtypeStruct((SENDS, 2, KROWS, LANES), F32),
            jax.ShapeDtypeStruct((SENDS + 1, WIDTH), F32),
        ),
        [block_level, part],
        [by_block(down_local), by_block(in_slot), by_block(shape_param), by_block(scale_param), sends],
        kernel_tables(),
        9_000_000_000,
        56 * 1024 * 1024,
    )


def composed_paths(days, ends, path_weights):
    return call(
        compose_kernel,
        jax.ShapeDtypeStruct((days + 8, WIDTH), F32),
        [],
        [ends, path_weights],
        [pltpu.VMEM((2, KROWS + days, LANES), F32)],
        1_000_000,
    )


def path_adjoints(pieces, gauge_ids, path_weights):
    shards = len(pieces)
    days = sum(piece.shape[0] for piece in pieces)
    return call(
        functools.partial(path_adjoint_kernel, shards),
        jax.ShapeDtypeStruct((days, WIDTH), F32),
        [],
        pieces + [gauge_ids, path_weights],
        [
            pltpu.VMEM((2 * days, pieces[0].shape[1]), BF16),
            pltpu.VMEM((SENDS, 2, days, LANES), F32),
            pltpu.VMEM((2, days + KROWS, LANES), F32),
        ],
        4_000_000_000,
    )


def reach_seeds(pieces, gauge_reach, gauge_ids, blocks):
    shards = len(pieces)
    days = sum(piece.shape[0] for piece in pieces)
    gauges = gauge_reach.shape[0]
    return call(
        functools.partial(seed_kernel, shards),
        jax.ShapeDtypeStruct((blocks, days, BLK), F32),
        [],
        pieces + [gauge_reach.reshape(1, gauges), gauge_ids],
        [pltpu.VMEM((2 * days, gauges), BF16), pltpu.VMEM((gauges, BLK), BF16)],
        3_000_000_000,
    )


def day_grads(inflow, shape_param, scale_param):
    own_days = inflow.shape[0]
    blocks = shape_param.shape[0] // BLK
    return call(
        grad_kernel,
        (
            jax.ShapeDtypeStruct((blocks, 2, KROWS, LANES), F32),
            jax.ShapeDtypeStruct((blocks, 2, 2 * own_days, BLK), F32),
        ),
        [],
        [inflow, by_block(shape_param), by_block(scale_param)],
        [pltpu.VMEM((2, own_days + 16, LANES), F32), pltpu.VMEM((2, 2, KROWS, LANES), F32)],
        1_000_000,
    )


def all_reaches(block_level, part, adjoints, composed, seeds, weights, grads, down_local, in_slot):
    own_days = grads.shape[2] // 2
    blocks, days = block_level.shape[0], seeds.shape[1]
    reaches = blocks * BLK
    return call(
        functools.partial(full_kernel, own_days),
        (jax.ShapeDtypeStruct((own_days, reaches), F32), jax.ShapeDtypeStruct((2, reaches), F32)),
        [block_level, part],
        [*adjoints, *composed, seeds, weights, grads, by_block(down_local), by_block(in_slot)],
        kernel_tables()
        + [
            pltpu.VMEM((2 * days, SENDS * WIDTH), BF16),
            pltpu.VMEM((2, days, LANES), F32),
            pltpu.VMEM((2, 2 * days, LANES), F32),
            pltpu.VMEM((2, days + KROWS, LANES), F32),
            pltpu.VMEM((2, 2 * days, MAXB * BLK), BF16),
        ],
        10_000_000_000,
    )


def after(values, *others):
    return lax.optimization_barrier((values, *others))[0]


def fast_shards(
    inflow, cotangent, gauge_reach, shape_param, scale_param, block_level, down_local, in_slot, send_reach,
):
    own_days = inflow.shape[0]
    blocks = block_level.shape[0]
    shards = lax.axis_size("tm")
    days = shards * own_days
    gauge_ids = gauge_columns(gauge_reach)
    part = after(lax.axis_index("basin").astype(jnp.int32).reshape(1), gauge_ids)
    path_weights, ends = sent_paths(
        block_level, part, shape_param, scale_param, down_local, in_slot, send_reach.reshape(SENDS, 1, KROWS)
    )
    back = lambda by, reach: [(i + by, i) for i in range(shards - reach)]
    following = lax.ppermute(cotangent, "tm", back(1, 1))
    following, ends, path_weights = lax.optimization_barrier((following, ends, path_weights))
    second = lax.ppermute(following, "tm", back(1, 2))
    third = lax.ppermute(following, "tm", back(2, 3))
    early = jnp.concatenate([cotangent, following], axis=0)
    path_weights = jnp.pad(path_weights, ((0, 1), (0, 0), (0, 0), (0, 0)))
    composed = composed_paths(days, ends, path_weights)[None]
    composed, own_inflow = lax.optimization_barrier((composed, inflow))
    weights, grads = day_grads(own_inflow, shape_param, scale_param)
    composed = jnp.concatenate([composed, exchange(composed, "basin", 2)], axis=0)
    composed, early, path_weights, grads = lax.optimization_barrier((composed, early, path_weights, grads))
    composed = jnp.concatenate([composed, exchange(composed, "basin", 4)], axis=0)
    composed = (composed, exchange(composed, "basin", 1))
    third, second, path_weights = lax.optimization_barrier((third, second, path_weights))
    pieces = [early, second, third]
    adjoints = path_adjoints(pieces, gauge_ids, path_weights)
    seeds = reach_seeds(pieces, gauge_reach, gauge_ids, blocks)
    adjoints = over_basin(adjoints, seeds)
    lateral, params = all_reaches(
        block_level, part, adjoints, composed, seeds, weights, grads, down_local, in_slot
    )
    first, second, third = (exchange(params, "tm", by) for by in (1, 2, 3))
    return lateral, (params + first) + (second + third)


def passed_along(shard, axis, by):
    peers = lax.axis_size(axis)
    pairs = [(i, i + by) for i in range(peers) if 0 <= i + by < peers]
    return lax.ppermute(shard, axis, pairs)


def kernel_of(shape_param, scale_param, lag_count):
    offsets = jnp.arange(lag_count, dtype=jnp.float32) + 0.5
    logits = (shape_param[None, :] - 1.0) * jnp.log(offsets)[:, None] - offsets[
        :, None
    ] / scale_param[None, :]
    weights = jnp.exp(logits)
    return (weights / jnp.sum(weights, axis=0, keepdims=True), offsets)


def lag_adjoint(kernel, extended, day_count):
    summed = kernel[0][None, :] * extended[0:day_count]
    for lag_index in range(1, kernel.shape[0]):
        summed = summed + kernel[lag_index][None, :] * extended[lag_index : lag_index + day_count]
    return summed


def lag_gradient(adjoint_in, inflow_ext, lag_count, day_count):
    per_lag = []
    for lag_index in range(lag_count):
        first_day = lag_count - 1 - lag_index
        per_lag.append(jnp.sum(adjoint_in * inflow_ext[first_day : first_day + day_count], axis=0))
    return jnp.stack(per_lag)


def param_terms(kernel, offsets, scale_param, kernel_grad):
    weighted = jnp.sum(kernel * kernel_grad, axis=0, keepdims=True)
    logit_grad = kernel * (kernel_grad - weighted)
    shape_grad = jnp.sum(logit_grad * jnp.log(offsets)[:, None], axis=0)
    scale_grad = jnp.sum(logit_grad * offsets[:, None], axis=0) / (scale_param * scale_param)
    return jnp.stack([shape_grad, scale_grad])


def take_blocks(values, chosen, block_count):
    rows = values.shape[0]
    picked = jnp.take(values.reshape(rows, block_count, BLK), chosen, axis=1)
    return picked.reshape(rows, chosen.shape[0] * BLK)


def inbound(seed_part, adjoint_all, received, below_reach, slot_of):
    local_part = jnp.where(
        below_reach[None, :] >= 0, adjoint_all[:, jnp.maximum(below_reach, 0)], 0.0
    )
    remote_part = jnp.where(slot_of[None, :] >= 0, received[:, jnp.maximum(slot_of, 0)], 0.0)
    return seed_part + local_part + remote_part


def shards(
    inflow,
    cotangent,
    gauge_reach,
    shape_param,
    scale_param,
    block_level,
    down_local,
    in_slot,
    send_reach,
):
    day_count, reach_count = inflow.shape
    lag_count = LAGS
    block_count = block_level.shape[0]
    kernel, offsets = kernel_of(shape_param, scale_param, lag_count)
    gauge_seed = jnp.zeros((day_count, reach_count), jnp.float32).at[:, gauge_reach].add(cotangent)
    earlier = passed_along(inflow[day_count - (lag_count - 1) :], "tm", 1)
    inflow_ext = jnp.concatenate([earlier, inflow], axis=0)
    adjoint_all = jnp.zeros((day_count, reach_count), jnp.float32)
    kernel_grad = jnp.zeros((lag_count, reach_count), jnp.float32)
    received = jnp.zeros((day_count, send_reach.shape[2]), jnp.float32)
    slot_ids = jnp.arange(MAXB, dtype=jnp.int32)
    block_ids = jnp.arange(block_count, dtype=jnp.int32)
    down_rows = down_local.reshape(1, reach_count)
    slot_rows = in_slot.reshape(1, reach_count)
    for height in range(LEVELS):
        at_height = block_level == height
        rank_of = jnp.cumsum(at_height.astype(jnp.int32)) - 1
        slot_hits = at_height[None, :] & (rank_of[None, :] == slot_ids[:, None])
        slot_valid = jnp.any(slot_hits, axis=1)
        chosen = jnp.sum(jnp.where(slot_hits, block_ids[None, :], 0), axis=1)
        below_reach = take_blocks(down_rows, chosen, block_count)[0]
        slot_of = take_blocks(slot_rows, chosen, block_count)[0]
        seed_part = take_blocks(gauge_seed, chosen, block_count)
        adjoint_in = inbound(seed_part, adjoint_all, received, below_reach, slot_of)
        later_head = passed_along(adjoint_in[: lag_count - 1], "tm", -1)
        extended = jnp.concatenate([adjoint_in, later_head], axis=0)
        outflow = lag_adjoint(take_blocks(kernel, chosen, block_count), extended, day_count)
        lag_grads = lag_gradient(
            adjoint_in, take_blocks(inflow_ext, chosen, block_count), lag_count, day_count
        )
        target_blocks = jnp.where(slot_valid, chosen, block_count)
        adjoint_all = (
            adjoint_all.reshape(day_count, block_count, BLK)
            .at[:, target_blocks]
            .set(outflow.reshape(day_count, MAXB, BLK), mode="drop")
            .reshape(day_count, reach_count)
        )
        kernel_grad = (
            kernel_grad.reshape(lag_count, block_count, BLK)
            .at[:, target_blocks]
            .set(lag_grads.reshape(lag_count, MAXB, BLK), mode="drop")
            .reshape(lag_count, reach_count)
        )
        if height + 1 < LEVELS:
            wanted = send_reach[0, height]
            outgoing = jnp.where(wanted[None, :] >= 0, adjoint_all[:, jnp.maximum(wanted, 0)], 0.0)
            received = lax.all_to_all(outgoing, "basin", split_axis=1, concat_axis=1, tiled=True)
    kernel_total = lax.psum(kernel_grad, "tm")
    param_grad = param_terms(kernel, offsets, scale_param, kernel_total)
    return (adjoint_all, param_grad)


def solution(mesh):
    in_specs = (
        P("tm", "basin"),
        P("tm", "basin"),
        P("basin"),
        P("basin"),
        P("basin"),
        P("basin"),
        P("basin"),
        P("basin"),
        P("basin", None, None),
    )
    out_specs = (P("tm", "basin"), P(None, "basin"))
    small = mesh.shape["basin"] == 8 and mesh.shape["tm"] == 4
    body = fast_shards if small else shards
    return jax.shard_map(body, mesh=mesh, in_specs=in_specs, out_specs=out_specs, check_vma=False)
```

```python
import functools

import jax
import jax.numpy as jnp
from jax import lax
from jax.experimental import pallas as pl
from jax.experimental.pallas import tpu as pltpu
from jax.sharding import PartitionSpec as P

BLK = 256
LAGS = 30
LEVELS = 8
MAXB = 4
LANES = 128
KROWS = 32
SENDS = LEVELS - 1
WIDTH = 2 * LANES
F32 = jnp.float32
BF16 = jnp.bfloat16
VMEM_LIMIT = 20 * 1024 * 1024
JOINT = 4


def iota(shape, axis):
    return lax.broadcasted_iota(jnp.int32, shape, axis)


def split_terms(values):
    high = values.astype(BF16)
    return high, (values - high.astype(F32)).astype(BF16)


def one_hot(hits):
    return jnp.where(hits, 1.0, 0.0).astype(BF16)


def product(left, right):
    return jnp.dot(left, right, preferred_element_type=F32)


def list_blocks(level_ref, order_ref, count_ref):
    for height in range(LEVELS):
        count_ref[height] = 0

    @pl.loop(0, level_ref.shape[0])
    def _(block):
        height = level_ref[block]
        rank = count_ref[height]
        order_ref[height * MAXB + rank] = block
        count_ref[height] = rank + 1


def lag_weights(shape_row, scale_row):
    rows = iota((KROWS, shape_row.shape[1]), 0)
    offsets = rows.astype(F32) + 0.5
    logs = jnp.log(offsets)
    weights = jnp.exp((shape_row - 1.0) * logs - offsets / scale_row)
    weights = jnp.where(rows < LAGS, weights, 0.0)
    return weights / jnp.sum(weights, axis=0, keepdims=True), offsets, logs


def lag_sum(buf, chunk, weight_of, days, lags=LAGS):
    total = jnp.zeros((days, LANES), F32)
    for shift in range(8):
        steps = [k for k in range(shift, lags, 8)]
        shifted = buf[chunk, pl.ds(shift, days + 8 * (len(steps) - 1)), :]
        for step, lag in enumerate(steps):
            total = total + weight_of(lag) * shifted[8 * step : 8 * step + days]
    return total


def lag_sum_forward(buf, chunk, weights_of, days):
    totals = [jnp.zeros((days, LANES), F32) for _ in weights_of]
    for shift in range(8):
        shifted = buf[chunk, pl.ds(8 - shift, days + 24), :]
        for step in range(4):
            lag = 8 * step + shift
            if lag < LAGS:
                part = shifted[24 - 8 * step : 24 - 8 * step + days]
                totals = [t + w(lag) * part for t, w in zip(totals, weights_of)]
    return totals


def path_kernel(
    level_ref, part_ref, down_ref, slot_ref, shape_ref, scale_ref, send_ref, weight_ref,
    ends_ref, order_ref, count_ref,
):
    list_blocks(level_ref, order_ref, count_ref)
    me = part_ref[0]
    width = WIDTH
    turn = me & 3
    halves = []
    for half in range(2):
        listed = [
            send_ref[h] if h < SENDS else jnp.full((1, KROWS), -1, jnp.int32)
            for h in range(4 * half, 4 * half + 4)
        ]
        listed = jnp.broadcast_to(jnp.concatenate(listed, axis=1), (8, LANES))
        halves.append(pltpu.roll(listed, turn * KROWS, 1)[0:1])
    want = jnp.concatenate(halves, axis=1)
    lane_id = iota((1, width), 1)
    want_level = (lane_id >> 7) * 4 + ((((lane_id & (LANES - 1)) >> 5) - turn) & 3)
    blank = jnp.zeros((4, BLK), F32)
    below = jnp.full((1, width), -1, jnp.int32)
    parent = jnp.full((1, width), -1, jnp.int32)
    rows = iota((BLK, width), 0)
    krows = iota((KROWS, width), 0)
    for height in range(SENDS - 1, -1, -1):
        node = jnp.where((want_level == height) & (want >= 0), want, below)

        def gather(index, total, node=node, height=height):
            block = order_ref[height * MAXB + index]
            hits = one_hot(rows == node - block * BLK)
            table = jnp.concatenate(
                [
                    down_ref[block].astype(F32),
                    slot_ref[block].astype(F32),
                    shape_ref[block],
                    scale_ref[block],
                    blank,
                ],
                axis=0,
            )
            high = table.astype(BF16)
            rest = table - high.astype(F32)
            middle = rest.astype(BF16)
            low = (rest - middle.astype(F32)).astype(BF16)
            return total + product(jnp.concatenate([high, middle, low, high * 0], axis=0), hits)

        found = lax.fori_loop(0, count_ref[height], gather, jnp.zeros((32, width), F32))
        found = (found[0:8] + found[8:16]) + found[16:24]
        active = node >= 0
        down = jnp.round(found[0:1]).astype(jnp.int32)
        slot = jnp.round(found[1:2]).astype(jnp.int32)
        shape_row = jnp.where(active, found[2:3], 2.0)
        scale_row = jnp.where(active, found[3:4], 2.0)
        ends = active & (slot >= 0)
        below = jnp.where(active & (down >= 0), down, -1)
        sender = slot >> 2
        lane = (sender >> 2) * LANES + ((sender + (height - 1)) & 3) * KROWS + me * 4 + (slot & 3)
        parent = jnp.where(ends, (height - 1) * width + lane, parent)
        weights = lag_weights(shape_row, scale_row)[0]
        weights = jnp.where(active, weights, jnp.where(krows == 0, 1.0, 0.0))
        weights = jnp.where(krows == KROWS - 1, node.astype(F32), weights)
        ends_ref[height : height + 1, :] = jnp.where(ends, 1.0, 0.0)
        for chunk in range(width // LANES):
            weight_ref[height, chunk] = weights[:, chunk * LANES : (chunk + 1) * LANES]
    ends_ref[SENDS : SENDS + 1, :] = parent.astype(F32)


def compose_kernel(ends_ref, weight_ref, comp_ref, buf_ref):
    width = ends_ref.shape[1]
    days = buf_ref.shape[1] - KROWS
    buf_ref[...] = jnp.zeros(buf_ref.shape, F32)
    first = iota((8, LANES), 0) == 0
    for height in range(1, SENDS):
        for chunk in range(height // 4, width // LANES):
            ends = ends_ref[height : height + 1, chunk * LANES : (chunk + 1) * LANES] > 0.5
            start = buf_ref[chunk, KROWS : KROWS + 8, :]
            buf_ref[chunk, KROWS : KROWS + 8, :] = jnp.where(first & ends, 1.0, start)

        @pl.loop(height // 4, width // LANES)
        def _(chunk, height=height):
            row = lambda lag: weight_ref[height, chunk, pl.ds(lag, 1), :]
            (total,) = lag_sum_forward(buf_ref, chunk, [row], days)
            buf_ref[chunk, KROWS : KROWS + days, :] = total

    for chunk in range(width // LANES):
        lanes = slice(chunk * LANES, (chunk + 1) * LANES)
        comp_ref[0:days, lanes] = buf_ref[chunk, KROWS : KROWS + days, :]
    comp_ref[days : days + 8, :] = jnp.broadcast_to(ends_ref[SENDS : SENDS + 1, :], (8, width))


def grad_kernel(inflow_ref, shape_ref, scale_ref, weight_ref, grad_ref, buf_ref, row_ref):
    days = inflow_ref.shape[0]
    buf_ref[...] = jnp.zeros(buf_ref.shape, F32)

    @pl.loop(0, weight_ref.shape[0])
    def _(block):
        scale_row = scale_ref[block]
        weights, offsets, logs = lag_weights(shape_ref[block], scale_row)
        by_shape = weights * (logs - jnp.sum(weights * logs, axis=0, keepdims=True))
        by_scale = weights * (offsets - jnp.sum(weights * offsets, axis=0, keepdims=True))
        by_scale = by_scale / (scale_row * scale_row)
        for chunk in range(2):
            lanes = slice(chunk * LANES, (chunk + 1) * LANES)
            weight_ref[block, chunk] = weights[:, lanes]
            row_ref[chunk, 0] = by_shape[:, lanes]
            row_ref[chunk, 1] = by_scale[:, lanes]
            at = pl.ds(pl.multiple_of(block * BLK + chunk * LANES, LANES), LANES)
            buf_ref[chunk, 8 : 8 + days, :] = inflow_ref[:, at]
        for chunk in range(2):
            lanes = slice(chunk * LANES, (chunk + 1) * LANES)
            totals = [[jnp.zeros((8, LANES), F32) for _ in range(days // 4)] for _ in range(2)]
            for shift in range(8):
                shifted = buf_ref[chunk, pl.ds(8 - shift, days + 8), :]
                for lag in range(shift, LAGS, 8):
                    for which, tiles in enumerate(totals):
                        weight = row_ref[chunk, which, lag : lag + 1, :]
                        for tile in range(days // 8 + 1):
                            at = tile + lag // 8
                            tiles[at] = tiles[at] + weight * shifted[8 * tile : 8 * tile + 8]
            for which, tiles in enumerate(totals):
                grad_ref[block, which, :, lanes] = jnp.concatenate(tiles, axis=0)


def gather_terms(pieces, terms_ref):
    days = terms_ref.shape[0] // 2
    start = 0
    for piece in pieces:
        high, low = split_terms(piece[...])
        end = start + piece.shape[0]
        terms_ref[start:end, :] = high
        terms_ref[days + start : days + end, :] = low
        start = end


def gauge_hits(gauge_ref, targets):
    return jnp.concatenate(
        [
            one_hot(gauge_ref[...] == targets[:, start : start + LANES])
            for start in range(0, targets.shape[1], LANES)
        ],
        axis=1,
    )


def folded(total):
    days = total.shape[0] // 2
    return total[:days] + total[days:]


def path_adjoint_kernel(shards, *refs):
    pieces = refs[:shards]
    gauge_ref, weight_ref, out_ref, terms_ref, seed_ref, buf_ref = refs[shards:]
    days = out_ref.shape[0]
    gather_terms(pieces, terms_ref)

    def fill(places):
        nodes = [weight_ref[height, chunk, KROWS - 1 : KROWS, :] for height, chunk in places]
        nodes = jnp.round(jnp.concatenate(nodes, axis=1)).astype(jnp.int32)
        seeds = folded(product(terms_ref[...], gauge_hits(gauge_ref, nodes)))
        for number, (height, chunk) in enumerate(places):
            seed_ref[height, chunk] = seeds[:, number * LANES : (number + 1) * LANES]

    @pl.loop(0, 4)
    def _(height):
        fill([(height, 0), (height, 1)])

    fill([(4, 1), (5, 1)])
    fill([(6, 1)])

    for chunk in range(2):
        buf_ref[chunk] = jnp.zeros(buf_ref.shape[1:], F32)

        @pl.loop(0, min(SENDS, 4 * chunk + 4))
        def _(height, chunk=chunk):
            buf_ref[chunk, 0:days, :] = buf_ref[chunk, 0:days, :] + seed_ref[height, chunk]
            row = lambda lag: weight_ref[height, chunk, pl.ds(lag, 1), :]
            buf_ref[chunk, 0:days, :] = lag_sum(buf_ref, chunk, row, days)

        out_ref[:, chunk * LANES : (chunk + 1) * LANES] = buf_ref[chunk, 0:days, :]


def seed_kernel(shards, *refs):
    pieces = refs[:shards]
    row_ref, gauge_ref, out_ref, terms_ref, hits_ref = refs[shards:]
    gather_terms(pieces, terms_ref)
    places = gauge_ref[...] & (BLK - 1)
    for chunk in range(2):
        lanes = iota((1, LANES), 1) + chunk * LANES
        hits_ref[:, chunk * LANES : (chunk + 1) * LANES] = one_hot(places == lanes)
    blocks = row_ref[...] // BLK

    rows = terms_ref.shape[0]

    @pl.loop(0, out_ref.shape[0] // JOINT)
    def _(group):
        masked = [terms_ref[...] * one_hot(blocks == group * JOINT + i) for i in range(JOINT)]
        total = product(jnp.concatenate(masked, axis=0), hits_ref[...])
        for i in range(JOINT):
            out_ref[group * JOINT + i] = folded(total[i * rows : (i + 1) * rows])


def full_kernel(
    own_days, level_ref, part_ref, a_own_ref, a_mate_ref, c_own_ref, c_mate_ref, seed_ref, weight_ref,
    grad_ref, down_ref, slot_ref, out_ref, param_ref,
    order_ref, count_ref, recv_ref, comp_ref, parent_buf, adj_ref, lat_ref,
):
    list_blocks(level_ref, order_ref, count_ref)
    me = part_ref[0]
    flip = (me >> 2) * LANES
    days = seed_ref.shape[1]
    width = 2 * LANES
    groups = iota((1, LANES), 1) >> 5
    rows = iota((BLK, width), 0)

    def merged(own_ref, mate_ref, height, half, at):
        lanes = slice((height // 4) * LANES, (height // 4 + 1) * LANES)
        total = None
        for ref, core in ((own_ref, 0), (mate_ref, 1)):
            for index in (2 * half, 2 * half + 1):
                sender = me ^ (core + 2 * index)
                part = ref[index, at, lanes]
                mine = groups == ((height + sender) & 3)
                total = part if total is None else jnp.where(mine, part, total)
        return total

    def days_of(height):
        return min(days, -(-(own_days + (LAGS - 1) * (LEVELS - 1 - height)) // 16) * 16)

    parent_buf[...] = jnp.zeros(parent_buf.shape, F32)
    for height in range(SENDS):
        if height:
            parents = jnp.concatenate(
                [
                    merged(c_own_ref, c_mate_ref, height, half, slice(days, days + 8))[0:1]
                    for half in range(2)
                ],
                axis=1,
            )
            parents = jnp.round(parents).astype(jnp.int32)
            parents = jnp.where(parents >= 0, parents ^ flip, -1)
            hits = jnp.concatenate(
                [one_hot(rows == parents - lower * width) for lower in range(height)], axis=0
            )
            total = product(recv_ref[:, 0 : height * width], hits)
            total = total[:days] + total[days:]
            for half in range(2):
                parent_buf[half, 0:days, :] = total[:, half * LANES : (half + 1) * LANES]
                comp_ref[half] = merged(c_own_ref, c_mate_ref, height, half, slice(0, days))
        lags = min(days, (LAGS - 1) * height + 1)
        for half in range(2):
            result = merged(a_own_ref, a_mate_ref, height, half, slice(0, days))
            if height:
                count = days_of(height) // 8
                tiles = [result[8 * i : 8 * i + 8] for i in range(days // 8)]
                for shift in range(8):
                    steps = [k for k in range(shift, lags, 8)]
                    for step, lag in enumerate(steps):
                        weight = comp_ref[half, lag : lag + 1, :]
                        for i in range(min(count, days // 8 - step)):
                            at = 8 * (i + step) + shift
                            tiles[i] = tiles[i] + weight * parent_buf[half, at : at + 8, :]
                result = jnp.concatenate(tiles, axis=0)
            high, low = split_terms(result)
            lanes = slice(height * width + half * LANES, height * width + (half + 1) * LANES)
            recv_ref[0:days, lanes] = high
            recv_ref[days : 2 * days, lanes] = low

    adj_ref[...] = jnp.zeros(adj_ref.shape, F32)
    lat_ref[...] = jnp.zeros(lat_ref.shape, BF16)

    def level(height, sources):
        need = days_of(height)
        have = days_of(height - 1) if height else days
        count = count_ref[height]

        def gather(rank):
            block = order_ref[height * MAXB + rank]
            seeds = seed_ref[block, 0:have, :]
            if not height:
                return seeds
            slot = slot_ref[block]
            sender = slot >> 2
            lane = ((sender >> 2) * LANES ^ flip) + ((sender + (height - 1)) & 3) * KROWS
            lane = jnp.where(slot >= 0, lane + me * 4 + (slot & 3), -1)
            down = down_ref[block]
            hits = [one_hot(rows == lane)]
            for index in range(sources):
                source = jnp.where(
                    index < count_ref[height - 1], order_ref[(height - 1) * MAXB + index], -2
                )
                hits.append(one_hot((rows == down - source * BLK) & (down >= 0)))
            terms = []
            for start, first in ((0, 0), (have, days)):
                local = lat_ref[(height - 1) % 2, start : start + have, 0 : sources * BLK]
                received = recv_ref[first : first + have, (height - 1) * width : height * width]
                terms.append(jnp.concatenate([received, local], axis=1))
            total = product(jnp.concatenate(terms, axis=0), jnp.concatenate(hits, axis=0))
            return seeds + total[:have] + total[have:]

        @pl.loop(0, count)
        def _(rank):
            adjoint = gather(rank)
            block = order_ref[height * MAXB + rank]
            for chunk in range(2):
                lanes = slice(chunk * LANES, (chunk + 1) * LANES)
                adj_ref[chunk, 0:have, :] = adjoint[:, lanes]
                at = pl.ds(pl.multiple_of(block * BLK + chunk * LANES, LANES), LANES)
                for which in range(2):
                    grads = adjoint[: 2 * own_days, lanes] * grad_ref[block, which, :, lanes]
                    param_ref[which : which + 1, at] = jnp.sum(grads, axis=0, keepdims=True)
                row = lambda lag, chunk=chunk: weight_ref[block, chunk, lag : lag + 1, :]
                result = lag_sum(adj_ref, chunk, row, need)
                out_ref[:, at] = result[:own_days]
                if height + 1 < LEVELS:
                    high, low = split_terms(result)
                    lanes = pl.ds(pl.multiple_of(rank * BLK + chunk * LANES, LANES), LANES)
                    lat_ref[height % 2, 0:need, lanes] = high
                    lat_ref[height % 2, need : 2 * need, lanes] = low

    level(0, 0)
    for height in range(1, LEVELS):
        few = count_ref[height - 1] <= MAXB // 2
        pl.when(few)(functools.partial(level, height, MAXB // 2))
        pl.when(jnp.logical_not(few))(functools.partial(level, height, MAXB))


def call(kernel, out_shape, in_smem, in_vmem, scratch, flops, limit=VMEM_LIMIT):
    vmem = pl.BlockSpec(memory_space=pltpu.VMEM)
    smem = pl.BlockSpec(memory_space=pltpu.SMEM)
    return pl.pallas_call(
        kernel,
        out_shape=out_shape,
        in_specs=[smem] * len(in_smem) + [vmem] * len(in_vmem),
        out_specs=jax.tree.map(lambda _: vmem, out_shape),
        scratch_shapes=scratch,
        compiler_params=pltpu.CompilerParams(vmem_limit_bytes=limit),
        cost_estimate=pl.CostEstimate(
            flops=flops,
            bytes_accessed=flops // 1000,
            transcendentals=0,
        ),
    )(*in_smem, *in_vmem)


def exchange(values, axis, by):
    return lax.ppermute(values, axis, [(i, i ^ by) for i in range(lax.axis_size(axis))])


def over_basin(values, *before):
    others = [exchange(values, "basin", by) for by in (2, 4, 6)]
    own = after(jnp.stack([values] + others), *before)
    return own, exchange(own, "basin", 1)


def gauge_columns(gauge_reach):
    return jnp.broadcast_to(gauge_reach[:, None], (gauge_reach.shape[0], LANES))


def kernel_tables():
    return [pltpu.SMEM((LEVELS * MAXB,), jnp.int32), pltpu.SMEM((LEVELS,), jnp.int32)]


def by_block(values):
    return values.reshape(-1, 1, BLK)


def sent_paths(block_level, part, shape_param, scale_param, down_local, in_slot, sends):
    return call(
        path_kernel,
        (
            jax.ShapeDtypeStruct((SENDS, 2, KROWS, LANES), F32),
            jax.ShapeDtypeStruct((SENDS + 1, WIDTH), F32),
        ),
        [block_level, part],
        [by_block(down_local), by_block(in_slot), by_block(shape_param), by_block(scale_param), sends],
        kernel_tables(),
        9_000_000_000,
        56 * 1024 * 1024,
    )


def composed_paths(days, ends, path_weights):
    return call(
        compose_kernel,
        jax.ShapeDtypeStruct((days + 8, WIDTH), F32),
        [],
        [ends, path_weights],
        [pltpu.VMEM((2, KROWS + days, LANES), F32)],
        1_000_000,
    )


def path_adjoints(pieces, gauge_ids, path_weights):
    shards = len(pieces)
    days = sum(piece.shape[0] for piece in pieces)
    return call(
        functools.partial(path_adjoint_kernel, shards),
        jax.ShapeDtypeStruct((days, WIDTH), F32),
        [],
        pieces + [gauge_ids, path_weights],
        [
            pltpu.VMEM((2 * days, pieces[0].shape[1]), BF16),
            pltpu.VMEM((SENDS, 2, days, LANES), F32),
            pltpu.VMEM((2, days + KROWS, LANES), F32),
        ],
        4_000_000_000,
    )


def reach_seeds(pieces, gauge_reach, gauge_ids, blocks):
    shards = len(pieces)
    days = sum(piece.shape[0] for piece in pieces)
    gauges = gauge_reach.shape[0]
    return call(
        functools.partial(seed_kernel, shards),
        jax.ShapeDtypeStruct((blocks, days, BLK), F32),
        [],
        pieces + [gauge_reach.reshape(1, gauges), gauge_ids],
        [pltpu.VMEM((2 * days, gauges), BF16), pltpu.VMEM((gauges, BLK), BF16)],
        3_000_000_000,
    )


def day_grads(inflow, shape_param, scale_param):
    own_days = inflow.shape[0]
    blocks = shape_param.shape[0] // BLK
    return call(
        grad_kernel,
        (
            jax.ShapeDtypeStruct((blocks, 2, KROWS, LANES), F32),
            jax.ShapeDtypeStruct((blocks, 2, 2 * own_days, BLK), F32),
        ),
        [],
        [inflow, by_block(shape_param), by_block(scale_param)],
        [pltpu.VMEM((2, own_days + 16, LANES), F32), pltpu.VMEM((2, 2, KROWS, LANES), F32)],
        1_000_000,
    )


def all_reaches(block_level, part, adjoints, composed, seeds, weights, grads, down_local, in_slot):
    own_days = grads.shape[2] // 2
    blocks, days = block_level.shape[0], seeds.shape[1]
    reaches = blocks * BLK
    return call(
        functools.partial(full_kernel, own_days),
        (jax.ShapeDtypeStruct((own_days, reaches), F32), jax.ShapeDtypeStruct((2, reaches), F32)),
        [block_level, part],
        [*adjoints, *composed, seeds, weights, grads, by_block(down_local), by_block(in_slot)],
        kernel_tables()
        + [
            pltpu.VMEM((2 * days, SENDS * WIDTH), BF16),
            pltpu.VMEM((2, days, LANES), F32),
            pltpu.VMEM((2, 2 * days, LANES), F32),
            pltpu.VMEM((2, days + KROWS, LANES), F32),
            pltpu.VMEM((2, 2 * days, MAXB * BLK), BF16),
        ],
        10_000_000_000,
    )


def after(values, *others):
    return lax.optimization_barrier((values, *others))[0]


def fast_shards(
    inflow, cotangent, gauge_reach, shape_param, scale_param, block_level, down_local, in_slot, send_reach,
):
    own_days = inflow.shape[0]
    blocks = block_level.shape[0]
    shards = lax.axis_size("tm")
    days = shards * own_days
    gauge_ids = gauge_columns(gauge_reach)
    part = after(lax.axis_index("basin").astype(jnp.int32).reshape(1), gauge_ids)
    path_weights, ends = sent_paths(
        block_level, part, shape_param, scale_param, down_local, in_slot, send_reach.reshape(SENDS, 1, KROWS)
    )
    back = lambda by, reach: [(i + by, i) for i in range(shards - reach)]
    following = lax.ppermute(cotangent, "tm", back(1, 1))
    following, ends, path_weights = lax.optimization_barrier((following, ends, path_weights))
    second = lax.ppermute(following, "tm", back(1, 2))
    third = lax.ppermute(following, "tm", back(2, 3))
    early = jnp.concatenate([cotangent, following], axis=0)
    path_weights = jnp.pad(path_weights, ((0, 1), (0, 0), (0, 0), (0, 0)))
    composed = composed_paths(days, ends, path_weights)[None]
    composed, own_inflow = lax.optimization_barrier((composed, inflow))
    weights, grads = day_grads(own_inflow, shape_param, scale_param)
    composed = jnp.concatenate([composed, exchange(composed, "basin", 2)], axis=0)
    composed, early, path_weights, grads = lax.optimization_barrier((composed, early, path_weights, grads))
    composed = jnp.concatenate([composed, exchange(composed, "basin", 4)], axis=0)
    composed = (composed, exchange(composed, "basin", 1))
    third, second, path_weights = lax.optimization_barrier((third, second, path_weights))
    pieces = [early, second, third]
    adjoints = path_adjoints(pieces, gauge_ids, path_weights)
    seeds = reach_seeds(pieces, gauge_reach, gauge_ids, blocks)
    adjoints = over_basin(adjoints, seeds)
    lateral, params = all_reaches(
        block_level, part, adjoints, composed, seeds, weights, grads, down_local, in_slot
    )
    first, second, third = (exchange(params, "tm", by) for by in (1, 2, 3))
    return lateral, (params + first) + (second + third)


def passed_along(shard, axis, by):
    peers = lax.axis_size(axis)
    pairs = [(i, i + by) for i in range(peers) if 0 <= i + by < peers]
    return lax.ppermute(shard, axis, pairs)


def kernel_of(shape_param, scale_param, lag_count):
    offsets = jnp.arange(lag_count, dtype=jnp.float32) + 0.5
    logits = (shape_param[None, :] - 1.0) * jnp.log(offsets)[:, None] - offsets[
        :, None
    ] / scale_param[None, :]
    weights = jnp.exp(logits)
    return (weights / jnp.sum(weights, axis=0, keepdims=True), offsets)


def lag_adjoint(kernel, extended, day_count):
    summed = kernel[0][None, :] * extended[0:day_count]
    for lag_index in range(1, kernel.shape[0]):
        summed = summed + kernel[lag_index][None, :] * extended[lag_index : lag_index + day_count]
    return summed


def lag_gradient(adjoint_in, inflow_ext, lag_count, day_count):
    per_lag = []
    for lag_index in range(lag_count):
        first_day = lag_count - 1 - lag_index
        per_lag.append(jnp.sum(adjoint_in * inflow_ext[first_day : first_day + day_count], axis=0))
    return jnp.stack(per_lag)


def param_terms(kernel, offsets, scale_param, kernel_grad):
    weighted = jnp.sum(kernel * kernel_grad, axis=0, keepdims=True)
    logit_grad = kernel * (kernel_grad - weighted)
    shape_grad = jnp.sum(logit_grad * jnp.log(offsets)[:, None], axis=0)
    scale_grad = jnp.sum(logit_grad * offsets[:, None], axis=0) / (scale_param * scale_param)
    return jnp.stack([shape_grad, scale_grad])


def take_blocks(values, chosen, block_count):
    rows = values.shape[0]
    picked = jnp.take(values.reshape(rows, block_count, BLK), chosen, axis=1)
    return picked.reshape(rows, chosen.shape[0] * BLK)


def inbound(seed_part, adjoint_all, received, below_reach, slot_of):
    local_part = jnp.where(
        below_reach[None, :] >= 0, adjoint_all[:, jnp.maximum(below_reach, 0)], 0.0
    )
    remote_part = jnp.where(slot_of[None, :] >= 0, received[:, jnp.maximum(slot_of, 0)], 0.0)
    return seed_part + local_part + remote_part


def shards(
    inflow,
    cotangent,
    gauge_reach,
    shape_param,
    scale_param,
    block_level,
    down_local,
    in_slot,
    send_reach,
):
    day_count, reach_count = inflow.shape
    lag_count = LAGS
    block_count = block_level.shape[0]
    kernel, offsets = kernel_of(shape_param, scale_param, lag_count)
    gauge_seed = jnp.zeros((day_count, reach_count), jnp.float32).at[:, gauge_reach].add(cotangent)
    earlier = passed_along(inflow[day_count - (lag_count - 1) :], "tm", 1)
    inflow_ext = jnp.concatenate([earlier, inflow], axis=0)
    adjoint_all = jnp.zeros((day_count, reach_count), jnp.float32)
    kernel_grad = jnp.zeros((lag_count, reach_count), jnp.float32)
    received = jnp.zeros((day_count, send_reach.shape[2]), jnp.float32)
    slot_ids = jnp.arange(MAXB, dtype=jnp.int32)
    block_ids = jnp.arange(block_count, dtype=jnp.int32)
    down_rows = down_local.reshape(1, reach_count)
    slot_rows = in_slot.reshape(1, reach_count)
    for height in range(LEVELS):
        at_height = block_level == height
        rank_of = jnp.cumsum(at_height.astype(jnp.int32)) - 1
        slot_hits = at_height[None, :] & (rank_of[None, :] == slot_ids[:, None])
        slot_valid = jnp.any(slot_hits, axis=1)
        chosen = jnp.sum(jnp.where(slot_hits, block_ids[None, :], 0), axis=1)
        below_reach = take_blocks(down_rows, chosen, block_count)[0]
        slot_of = take_blocks(slot_rows, chosen, block_count)[0]
        seed_part = take_blocks(gauge_seed, chosen, block_count)
        adjoint_in = inbound(seed_part, adjoint_all, received, below_reach, slot_of)
        later_head = passed_along(adjoint_in[: lag_count - 1], "tm", -1)
        extended = jnp.concatenate([adjoint_in, later_head], axis=0)
        outflow = lag_adjoint(take_blocks(kernel, chosen, block_count), extended, day_count)
        lag_grads = lag_gradient(
            adjoint_in, take_blocks(inflow_ext, chosen, block_count), lag_count, day_count
        )
        target_blocks = jnp.where(slot_valid, chosen, block_count)
        adjoint_all = (
            adjoint_all.reshape(day_count, block_count, BLK)
            .at[:, target_blocks]
            .set(outflow.reshape(day_count, MAXB, BLK), mode="drop")
            .reshape(day_count, reach_count)
        )
        kernel_grad = (
            kernel_grad.reshape(lag_count, block_count, BLK)
            .at[:, target_blocks]
            .set(lag_grads.reshape(lag_count, MAXB, BLK), mode="drop")
            .reshape(lag_count, reach_count)
        )
        if height + 1 < LEVELS:
            wanted = send_reach[0, height]
            outgoing = jnp.where(wanted[None, :] >= 0, adjoint_all[:, jnp.maximum(wanted, 0)], 0.0)
            received = lax.all_to_all(outgoing, "basin", split_axis=1, concat_axis=1, tiled=True)
    kernel_total = lax.psum(kernel_grad, "tm")
    param_grad = param_terms(kernel, offsets, scale_param, kernel_total)
    return (adjoint_all, param_grad)


def solution(mesh):
    in_specs = (
        P("tm", "basin"),
        P("tm", "basin"),
        P("basin"),
        P("basin"),
        P("basin"),
        P("basin"),
        P("basin"),
        P("basin"),
        P("basin", None, None),
    )
    out_specs = (P("tm", "basin"), P(None, "basin"))
    small = mesh.shape["basin"] == 8 and mesh.shape["tm"] == 4
    body = fast_shards if small else shards
    return jax.shard_map(body, mesh=mesh, in_specs=in_specs, out_specs=out_specs, check_vma=False)
```
